256 devices in a mesh: seq: 16 (over x_lo, z), expert: 16 (over x_hi, y, core).
Axes of the slice: x: 4 (x_hi: 2, x_lo: 2; x = x_hi * 2 + x_lo), y: 4, z: 8, core: 2. Of those that a mesh axis runs over, the one named last changes fastest.
Arguments:
- queries: bfloat16 [2048, 2, 8192], P('seq', None, 'expert'), may hold values from -8 to 8
- keys: bfloat16 [2048, 2, 512], P('seq'), may hold values from -8 to 8
- values: bfloat16 [2048, 2, 512], P('seq'), may hold values from -6 to 6
- prefix_keys: bfloat16 [64, 512], replicated, may hold values from -6 to 6
- prefix_values: bfloat16 [64, 512], replicated, may hold values from -6 to 6
- out_weight: bfloat16 [8192, 4096], P('expert', 'seq'), may hold values from -0.0625 to 0.0625
- residual_in: bfloat16 [2048, 2, 4096], P(('seq', 'expert')), may hold values from -8 to 8
- norm_gain: bfloat16 [4096], replicated, may hold values from 0.25 to 1.75
- expert_ids: int32 [2048, 2, 8], P(('seq', 'expert')), may hold values from 0 to 63, all different within a row; in each aligned block of 16 rows (0 to 15, 16 to 31, ..., all dimensions but the last counted through in order) at most 3 rows name the same one
- route_weights: float32 [2048, 2, 8], P(('seq', 'expert')), may hold values from 0.05 to 1
- w_gate: bfloat16 [16, 16, 4096, 384], P('seq', 'expert'), may hold values from -0.09375 to 0.09375
- w_up: bfloat16 [16, 16, 4096, 384], P('seq', 'expert'), may hold values from -0.09375 to 0.09375
- w_down: bfloat16 [16, 16, 384, 4096], P('seq', 'expert'), may hold values from -0.15625 to 0.15625
Outputs:
- mixed: bfloat16 [2048, 2, 4096], P(('seq', 'expert'))
The draws below stay inside these ranges and needn't reach their ends.
Inputs may be any that keep to these rules, and one draw needn't show every extreme that they name: `expert_ids`: each token names 8 different experts; among the 16 tokens of one device (aligned blocks of 16 rows in position then sequence order) no expert is named more than 3 times.
All inputs are finite; a program needn't handle non-finite values.
Results may differ from the reference program's by a relative error of at most 0.019.
Values may be sent and summed in bfloat16 or wider, within the bound.
A program may use at most 128 MiB of HBM per device.

```python
import math
import jax
import jax.numpy as jnp
import numpy as np
from jax import lax

D = 4096
HD = 128
KV = 4
FF = 1536
HQ_DEV = 4
EXP_DEV = 4
TOPK = 8
PREFIX = 64
SEQS = 2
TOKX = 16
HEADS = 64
EXPERTS = 64
SLICES = 4
FF_SLICE = 384
L = 2048
CAP = 3
N_SEQ = 16
N_EXPERT = 16


def draw_queries(key, part):
    key = jax.random.fold_in(key, 3)
    sample_field = jnp.clip(1.5 * jax.random.normal(key, (L, SEQS, HEADS * HD), jnp.float32), -6.0, 6.0)
    return sample_field.astype(jnp.bfloat16)


def draw_keys(key, part):
    key = jax.random.fold_in(key, 7)
    sample_field = jnp.clip(1.5 * jax.random.normal(key, (L, SEQS, KV * HD), jnp.float32), -6.0, 6.0)
    return sample_field.astype(jnp.bfloat16)


def draw_residual_in(key, part):
    key = jax.random.fold_in(key, 5)
    row_key, column_key, value_key = jax.random.split(key, 3)
    row_scale = jnp.exp(jax.random.uniform(row_key, (L, SEQS, 1), jnp.float32, math.log(0.2), math.log(2.0)))
    column_scale = jnp.exp(jax.random.uniform(column_key, (D,), jnp.float32, math.log(0.3), math.log(3.0)))
    base_field = jax.random.normal(value_key, (L, SEQS, D), jnp.float32)
    return jnp.clip(base_field * row_scale * column_scale, -8.0, 8.0).astype(jnp.bfloat16)


def shard_levels(own_key, shape, pieces, least, top_value):
    def one(dim, blocks):
        heights = jax.random.uniform(jax.random.fold_in(jax.random.fold_in(own_key, 6), dim), (blocks,), jnp.float32, least / len(pieces), top_value / len(pieces))
        return jnp.repeat(jnp.exp(heights), shape[dim] // blocks).reshape((-1,) + (1,) * (len(shape) - dim - 1))

    level = one(*pieces[0])
    for cut in pieces[1:]:
        level = level * one(*cut)
    return level


def routed_block(own_key, own, number, rows, count, top, reach, lean):
    sequence = jax.random.permutation(own_key, count)
    heavy_load, usual = shares(count, rows * top, reach, lean, True), shares(count, rows * top, reach, lean, False)
    places = jnp.arange(count)

    def named(lengths, rotation):
        used = int((lengths > 0).sum())
        fixed = max(1, used // 4)
        passed = fixed + (places - fixed + rotation * (used - fixed)) % max(1, count - fixed)
        return jnp.zeros((count,), jnp.int32).at[sequence[jnp.where(places < fixed, places, passed)]].set(jnp.asarray(lengths, jnp.int32))

    lengths = jnp.where(number % 4 == 0, named(heavy_load, number // 4), named(usual, number - number // 4 - 1))
    mixed = jax.random.permutation(jax.random.fold_in(own, 3), count)
    source_of, taker = mixed[0:count // 2 * 2:2], mixed[1:count // 2 * 2:2]
    margin = jnp.minimum(lengths[source_of] - 1, reach - lengths[taker]) // 2
    margin = jnp.where((source_of == sequence[0]) | (taker == sequence[0]) | (lengths[taker] == 0), 0, jnp.maximum(margin, 0))
    passed = jax.random.randint(jax.random.fold_in(own, 4), (count // 2,), 0, 1 << 20) % (margin + 1)
    lengths = lengths.at[source_of].add(-passed).at[taker].add(passed)
    items = jnp.searchsorted(jnp.cumsum(lengths), jnp.arange(rows * top), side="right").astype(jnp.int32)
    listing = items.reshape(top, rows).T
    listing = listing[jax.random.permutation(jax.random.fold_in(own, 1), rows)]
    rotation = jax.random.randint(jax.random.fold_in(own, 2), (rows, 1), 0, top)
    return jnp.take_along_axis(listing, (jnp.arange(top)[None, :] + rotation) % top, axis=1)


def shares(number_of, total, limit, skew, full):
    portions = [(1 << 20) // math.isqrt(rank ** skew) + 1 for rank in range(1, number_of + 1)]
    largest = limit if full else min(limit, max(-(-total // number_of), total * portions[0] // sum(portions)))
    least = 1 if total - largest >= number_of - 1 else 0
    given, surplus = [largest] + [least] * (number_of - 1), total - largest - least * (number_of - 1)
    while surplus > 0:
        movable = [i for i in range(1, number_of) if given[i] < largest] or [i for i in range(1, number_of) if given[i] < limit]
        whole, left = sum([portions[i] for i in movable]), surplus
        for i in movable:
            addition = min(limit - given[i], max(1, left * portions[i] // whole), surplus)
            given[i] = given[i] + addition
            surplus = surplus - addition
    return np.array(given)


def normal_values(key, dims, scale, most, shards=(), kind=jnp.bfloat16):
    loudness = shard_levels(key, dims, shards, -0.22, 0.18) if shards else 1.0
    drawn = jax.random.normal(key, dims, jnp.float32) * scale * loudness
    return jnp.minimum(jnp.maximum(drawn, -most), most).astype(kind)


def setup_inputs(seed: int = 0) -> dict:
    splits = jax.random.split(jax.random.key(seed), 14)
    queries = draw_queries(jax.random.fold_in(splits[13], 71), 0)
    keys = draw_keys(jax.random.fold_in(splits[13], 71), 0)
    values = normal_values(splits[2], (L, SEQS, KV * HD), 1.0, 6.0, ((0, 16),))
    prefix_keys = normal_values(splits[3], (PREFIX, KV * HD), 1.5, 6.0)
    prefix_values = normal_values(splits[4], (PREFIX, KV * HD), 1.0, 6.0)
    out_weight = normal_values(splits[5], (HEADS * HD, D), (HEADS * HD) ** -0.5, 0.0625, ((0, 16), (1, 16)))
    residual_in = draw_residual_in(jax.random.fold_in(splits[13], 71), 0)
    norm_gain = jnp.clip(1.0 + 0.15 * jax.random.normal(splits[7], (D,), jnp.float32), 0.25, 1.75).astype(jnp.bfloat16)
    expert_ids_keys = jax.random.split(jax.random.fold_in(splits[8], 1), L * SEQS // TOKX)
    expert_ids_turns = jax.random.permutation(jax.random.fold_in(splits[8], 3), L * SEQS // TOKX)
    expert_ids = jax.vmap(lambda own, number: routed_block(jax.random.fold_in(splits[8], 2), own, number, TOKX, EXPERTS, TOPK, CAP, 2))(expert_ids_keys, expert_ids_turns).reshape((L, SEQS, TOPK))
    route_weights = jnp.clip(jnp.exp(math.log(1.0) - 2.9957323 * jax.random.uniform(splits[9], (L, SEQS, TOPK), jnp.float32) ** shard_levels(splits[9], (L, SEQS, TOPK), ((0, 256),), -0.2, 0.2)), 0.05, 1.0)
    w_gate = normal_values(splits[10], (EXP_DEV * SLICES, N_EXPERT, D, FF_SLICE), D ** -0.5, 0.09375, ((0, 16), (1, 16)))
    w_up = normal_values(splits[11], (EXP_DEV * SLICES, N_EXPERT, D, FF_SLICE), D ** -0.5, 0.09375, ((0, 16), (1, 16)))
    w_down = normal_values(splits[12], (EXP_DEV * SLICES, N_EXPERT, FF_SLICE, D), FF ** -0.5, 0.15625, ((0, 16), (1, 16)))
    return {"queries": queries, "keys": keys, "values": values, "prefix_keys": prefix_keys, "prefix_values": prefix_values, "out_weight": out_weight, "residual_in": residual_in, "norm_gain": norm_gain, "expert_ids": expert_ids, "route_weights": route_weights, "w_gate": w_gate, "w_up": w_up, "w_down": w_down}


def attend(queries, keys, values, prefix_keys, prefix_values):
    head_group = HEADS // KV
    score_scale = 1.0 / math.sqrt(HD)
    places = jnp.arange(L, dtype=jnp.int32)
    causal = places[None, :] <= places[:, None]

    def one_head(head_index):
        shared_head = head_index // head_group
        query_head = lax.dynamic_slice_in_dim(queries, head_index * HD, HD, 2).astype(jnp.float32)
        key_head = lax.dynamic_slice_in_dim(keys, shared_head * HD, HD, 2).astype(jnp.float32)
        value_head = lax.dynamic_slice_in_dim(values, shared_head * HD, HD, 2).astype(jnp.float32)
        prefix_key = lax.dynamic_slice_in_dim(prefix_keys, shared_head * HD, HD, 1).astype(jnp.float32)
        prefix_value = lax.dynamic_slice_in_dim(prefix_values, shared_head * HD, HD, 1).astype(jnp.float32)
        main_scores = jnp.einsum('ibd,jbd->bij', query_head, key_head) * score_scale
        main_scores = jnp.where(causal[None], main_scores, -1e+30)
        prefix_scores = jnp.einsum('ibd,pd->bip', query_head, prefix_key) * score_scale
        row_top = jnp.maximum(lax.optimization_barrier(jnp.max(main_scores, -1)), lax.optimization_barrier(jnp.max(prefix_scores, -1)))
        main_probs = lax.optimization_barrier(jnp.exp(main_scores - row_top[..., None]).astype(jnp.bfloat16)).astype(jnp.float32)
        prefix_probs = lax.optimization_barrier(jnp.exp(prefix_scores - row_top[..., None]).astype(jnp.bfloat16)).astype(jnp.float32)
        row_total = lax.optimization_barrier(jnp.sum(main_probs, -1)) + lax.optimization_barrier(jnp.sum(prefix_probs, -1))
        weighted = jnp.einsum('bij,jbd->bid', main_probs, value_head) + jnp.einsum('bip,pd->bid', prefix_probs, prefix_value)
        return weighted / row_total[..., None]
    heads_out = lax.map(one_head, jnp.arange(HEADS, dtype=jnp.int32))
    return jnp.transpose(heads_out, (2, 1, 0, 3)).reshape(L, SEQS, HEADS * HD).astype(jnp.bfloat16)

def project(attended, out_weight):
    group_width = HQ_DEV * HD
    flat_rows = attended.reshape(L * SEQS, HEADS * HD)

    def add_group(running, group_index):
        group_part = lax.dynamic_slice_in_dim(flat_rows, group_index * group_width, group_width, 1)
        group_rows = lax.dynamic_slice_in_dim(out_weight, group_index * group_width, group_width, 0)
        term_rows = jnp.dot(group_part, group_rows, preferred_element_type=jnp.float32)
        term_rows = lax.optimization_barrier(term_rows.astype(jnp.bfloat16)).astype(jnp.float32)
        return (running + term_rows, None)
    running, unused = lax.scan(add_group, jnp.zeros((L * SEQS, D), jnp.float32), jnp.arange(N_EXPERT, dtype=jnp.int32))
    return running

def run_experts(normed, expert_ids, route_weights, w_gate, w_up, w_down):
    routes = expert_ids.reshape(-1)
    weights = route_weights.reshape(-1).astype(jnp.float32)
    route_count = routes.shape[0]
    most_rows = N_SEQ * N_EXPERT * CAP
    slot_range = jnp.arange(most_rows, dtype=jnp.int32)

    def one_expert(running, expert):
        chosen = routes == expert
        rank_in = jnp.cumsum(chosen.astype(jnp.int32)) - 1
        target = jnp.where(chosen, rank_in, most_rows)
        picked = jnp.zeros((most_rows,), jnp.int32).at[target].set(jnp.arange(route_count, dtype=jnp.int32), mode='drop')
        filled = slot_range < jnp.sum(chosen.astype(jnp.int32))
        tokens = picked // TOPK
        inputs = normed[tokens]
        column = expert // EXP_DEV
        within = expert % EXP_DEV
        output = jnp.zeros((most_rows, D), jnp.float32)
        for block_index in range(SLICES):
            entry_index = within * SLICES + block_index
            gate_proj = jnp.dot(inputs, w_gate[entry_index, column], preferred_element_type=jnp.float32)
            up_proj = jnp.dot(inputs, w_up[entry_index, column], preferred_element_type=jnp.float32)
            hidden = (jax.nn.silu(gate_proj) * up_proj).astype(jnp.bfloat16)
            block_out = jnp.dot(hidden, w_down[entry_index, column], preferred_element_type=jnp.float32)
            output = output + lax.optimization_barrier(block_out.astype(jnp.bfloat16)).astype(jnp.float32)
        output = lax.optimization_barrier(output.astype(jnp.bfloat16)).astype(jnp.float32)
        scaled = output * jnp.where(filled, weights[picked], 0.0)[:, None]
        return (running.at[tokens].add(scaled), None)
    running, unused = lax.scan(one_expert, jnp.zeros((L * SEQS, D), jnp.float32), jnp.arange(EXPERTS, dtype=jnp.int32))
    return running

def reference(queries, keys, values, prefix_keys, prefix_values, out_weight, residual_in, norm_gain, expert_ids, route_weights, w_gate, w_up, w_down):
    attended = attend(queries, keys, values, prefix_keys, prefix_values)
    hidden_state = residual_in.reshape(L * SEQS, D).astype(jnp.float32) + project(attended, out_weight)
    square = lax.optimization_barrier(jnp.mean(hidden_state * hidden_state, -1, keepdims=True))
    normed = (hidden_state * lax.rsqrt(square + 1e-06) * norm_gain.astype(jnp.float32)).astype(jnp.bfloat16)
    expert_mix = run_experts(normed, expert_ids, route_weights, w_gate, w_up, w_down)
    return (hidden_state + expert_mix).astype(jnp.bfloat16).reshape(L, SEQS, D)
```

```python
import math

import jax
import jax.numpy as jnp
from jax import lax
from jax.experimental import pallas as pl
from jax.experimental.pallas import tpu as pltpu
from jax.sharding import PartitionSpec as P

D = 4096
HD = 128
KV = 4
EXP_DEV = 4
TOPK = 8


MESH = pl.DeviceIdType.MESH
BF = jnp.bfloat16
F32 = jnp.float32
NT = (((1,), (1,)), ((), ()))
ORDER = (0, 1, 3, 2)
SPOS = {0: 0, 1: 1, 3: 2, 2: 3}
MOE_SEMS = 160


def place():
    s = lax.axis_index("seq")
    e = lax.axis_index("expert")
    return (e // 8) * 2 + s // 8, (e // 2) % 4, s % 8, e % 2


def device(x, y, z, c):
    return ((x % 2) * 8 + z, ((x // 2) * 4 + y) * 2 + c)


class Links:
    def __init__(self, send_sems, recv_sems):
        self.send_sems = send_sems
        self.recv_sems = recv_sems
        self.used = 0
        self.open = []

    def send(self, src, dst, peer):
        index = self.used
        self.used += 1
        copy = pltpu.make_async_remote_copy(
            src_ref=src,
            dst_ref=dst,
            send_sem=self.send_sems.at[index],
            recv_sem=self.recv_sems.at[index],
            device_id=peer,
            device_id_type=MESH,
        )
        copy.start()
        self.open.append(copy)
        return copy

    def finish(self):
        for copy in self.open:
            copy.wait_send()
        self.open = []


def greet(peers):
    barrier = pltpu.get_barrier_semaphore()
    for peer in peers:
        pl.semaphore_signal(barrier, inc=1, device_id=peer, device_id_type=MESH)
    return lambda: pl.semaphore_wait(barrier, len(peers))


def moe_kernel(
    normed,
    ids,
    gates,
    w_gate,
    w_up,
    w_down,
    out,
    tok,
    stage,
    tok_a,
    tok_b,
    slot_a,
    slot_b,
    got_a,
    got_b,
    back_a,
    back_b,
    acc,
    hid,
    w_in,
    w_out,
    rank_mask,
    rank_mask_t,
    half_send,
    half_recv,
    part_send,
    part_recv,
    total,
    z_send,
    z_plus,
    z_minus,
    core_send,
    core_recv,
    send_sems,
    recv_sems,
    local_sems,
):
    x, y, z, core = place()
    other = 1 - core

    def at(dx=0, dy=0, dz=0, dc=0):
        return device((x + dx) % 4, (y + dy) % 4, (z + dz) % 8, (core + dc) % 2)

    sibling = at(dc=1)
    peers = [sibling, at(dz=1), at(dz=7)]
    for d in (1, 2, 3):
        for dc in (0, 1):
            peers.append(at(dx=d, dc=dc))
            peers.append(at(dy=d, dc=dc))
    arrived = greet(peers)
    loads = [
        pltpu.make_async_copy(w_gate, w_in.at[:, 0:384], local_sems.at[0]),
        pltpu.make_async_copy(w_up, w_in.at[:, 384:768], local_sems.at[1]),
        pltpu.make_async_copy(w_down, w_out, local_sems.at[2]),
    ]
    for load in loads:
        load.start()

    lane = lax.broadcasted_iota(jnp.int32, (16, 128), 1)
    chosen = jnp.zeros((16, 128), F32)
    weight = jnp.zeros((16, 128), F32)
    for j in range(TOPK):
        column = ids[:, j : j + 1]
        chosen = chosen + jnp.where(lane == column, 1.0, 0.0)
        weight = weight + jnp.where(lane == column + 64, gates[:, j : j + 1], 0.0)
    row_i = lax.broadcasted_iota(jnp.int32, (16, 16), 0)
    col_i = lax.broadcasted_iota(jnp.int32, (16, 16), 1)
    lower = jnp.where(col_i <= row_i, 1.0, 0.0).astype(BF)
    rank = jnp.dot(lower, chosen.astype(BF), preferred_element_type=F32)
    meta = (rank * chosen + weight).astype(BF)

    own_rows = pl.ds(pl.multiple_of(core * 16, 16), 16)

    def columns(k, h):
        return pl.ds(pl.multiple_of(k * 2048 + h * 1024, 1024), 1024)

    stage[:, 0:1024] = normed[:, columns(other, 0)]
    stage[:, 1024:1152] = meta
    stage[:, 1152:2176] = normed[:, columns(other, 1)]
    tok[own_rows, 0:1024] = normed[:, columns(core, 0)]
    tok[own_rows, 1024:1152] = meta
    tok[own_rows, 1152:2176] = normed[:, columns(core, 1)]

    links = Links(send_sems, recv_sems)
    arrived()
    links.send(stage, tok.at[own_rows], sibling).wait_recv()

    def rows(dz):
        return pl.ds(dz * 32, 32)

    dense = {}

    def spread(dz):
        r = rows(dz)
        dense["a3", dz] = links.send(tok.at[r, 0:1152], tok_a.at[3, r], at(dx=1))
        dense["b3", dz] = links.send(tok.at[r, 1024:2176], tok_b.at[3, r], at(dy=1))
        dense["a1", dz] = links.send(tok.at[r, 0:1152], tok_a.at[1, r], at(dx=3))
        dense["b1", dz] = links.send(tok.at[r, 1024:2176], tok_b.at[1, r], at(dy=3))

    def relay_up(dz):
        r = rows(dz)
        dense["a3", dz].wait_recv()
        dense["a2", dz] = links.send(tok_a.at[3, r], tok_a.at[2, r], at(dx=1))
        dense["b3", dz].wait_recv()
        dense["b2", dz] = links.send(tok_b.at[3, r], tok_b.at[2, r], at(dy=1))

    def relay_down(dz):
        r = rows(dz)
        dense["a1", dz].wait_recv()
        dense["a2", dz] = links.send(tok_a.at[1, r], tok_a.at[2, r], at(dx=3))
        dense["b1", dz].wait_recv()
        dense["b2", dz] = links.send(tok_b.at[1, r], tok_b.at[2, r], at(dy=3))

    z_up, z_down = at(dz=1), at(dz=7)
    up = links.send(tok.at[rows(0)], tok.at[rows(7)], z_up)
    down = links.send(tok.at[rows(0)], tok.at[rows(1)], z_down)
    spread(0)

    n = lax.broadcasted_iota(jnp.int32, (8, 48, 256), 1)
    t = lax.broadcasted_iota(jnp.int32, (8, 48, 256), 2)
    block = (n * 171) >> 9
    rank_mask[...] = (
        jnp.where(block == (t >> 4), n - 3 * block + 1, -1).astype(F32).reshape(384, 256)
    )
    r = lax.broadcasted_iota(jnp.int32, (256, 384), 1)
    t = lax.broadcasted_iota(jnp.int32, (256, 384), 0)
    n = r - 48 * ((r * 1366) >> 16)
    block = (n * 171) >> 9
    rank_mask_t[...] = jnp.where(block == (t >> 4), n - 3 * block + 1, -1).astype(F32)

    q = lax.broadcasted_iota(jnp.int32, (8, 48, 128), 0)
    lane = lax.broadcasted_iota(jnp.int32, (8, 48, 128), 2)
    step = q >> 1
    to_core = (core + (q & 1)) & 1
    to_y = (y + step) & 3
    to_x = (x + step) & 3
    half = z // 4
    expert_a = 4 * ((x // 2 * 4 + to_y) * 2 + to_core) + 2 * (x % 2) + half
    expert_b = 4 * (((to_x >> 1) * 4 + y) * 2 + to_core) + 2 * (to_x & 1) + half
    pick_a = jnp.where(lane == expert_a, 1.0, 0.0).astype(BF).reshape(384, 128)
    pick_b = jnp.where(lane == expert_b, 1.0, 0.0).astype(BF).reshape(384, 128)
    pick_aw = jnp.where(lane == expert_a + 64, 1.0, 0.0).astype(BF).reshape(384, 128)
    pick_bw = jnp.where(lane == expert_b + 64, 1.0, 0.0).astype(BF).reshape(384, 128)

    up.wait_recv()
    up = links.send(tok.at[rows(7)], tok.at[rows(6)], z_up)
    down.wait_recv()
    down = links.send(tok.at[rows(1)], tok.at[rows(2)], z_down)
    spread(7)
    spread(1)
    relay_up(0)
    up.wait_recv()
    up = links.send(tok.at[rows(6)], tok.at[rows(5)], z_up)
    down.wait_recv()
    down = links.send(tok.at[rows(2)], tok.at[rows(3)], z_down)
    spread(6)
    spread(2)
    relay_up(7)
    relay_down(1)
    up.wait_recv()
    up = links.send(tok.at[pl.ds(5 * 32, 16)], tok.at[pl.ds(4 * 32, 16)], z_up)
    down.wait_recv()
    down = links.send(tok.at[pl.ds(3 * 32 + 16, 16)], tok.at[pl.ds(4 * 32 + 16, 16)], z_down)
    spread(5)
    spread(3)
    relay_up(6)
    relay_down(2)
    up.wait_recv()
    down.wait_recv()
    spread(4)
    relay_up(5)
    relay_down(3)

    def tokens(h, d):
        if d == 0:
            return tok[:, 0:1024] if h == 0 else tok[:, 1152:2176]
        return tok_a[d, :, 0:1024] if h == 0 else tok_b[d, :, 128:1152]

    def metas(h, d):
        if d == 0:
            return tok[:, 1024:1152]
        return tok_a[d, :, 1024:1152] if h == 0 else tok_b[d, :, 0:128]

    slot = (slot_a, slot_b)
    got = (got_a, got_b)
    back = (back_a, back_b)
    pick = (pick_a, pick_b)
    pick_w = (pick_aw, pick_bw)

    def select(h, d):
        found = lax.dot_general(pick[h], metas(h, d), NT, preferred_element_type=F32)
        chosen = jnp.where(found == rank_mask[...], 1.0, 0.0).astype(BF)
        picked = jnp.dot(chosen, tokens(h, d), preferred_element_type=F32)
        slot[h][SPOS[d]] = picked.astype(BF).reshape(8, 48, 1024)

    def toward(h, d, dc):
        return at(dx=d, dc=dc) if h else at(dy=d, dc=dc)

    moved = {}
    kept = {}

    def dispatch(h, part):
        span = pl.ds(0, 3) if part == 0 else pl.ds(3, 1)
        for d in (2, 1, 3, 0):
            for dc in (0, 1):
                src = slot[h].at[span, d * 2 + dc]
                dst = got[h].at[((4 - d) % 4) * 2 + dc, span]
                if d == 0 and dc == 0:
                    copy = pltpu.make_async_copy(src, dst, local_sems.at[3 + h * 2 + part])
                    copy.start()
                    kept[h, part] = copy
                else:
                    moved[h, part, d, dc] = links.send(src, dst, toward(h, d, dc))

    select(0, 0)
    select(1, 0)
    for dz in range(8):
        if dz not in (0, 7, 6, 5):
            dense["a3", dz].wait_recv()
            dense["b3", dz].wait_recv()
        if dz not in (1, 2, 3, 4):
            dense["a1", dz].wait_recv()
            dense["b1", dz].wait_recv()
        if dz == 4:
            relay_down(4)
    for h in (0, 1):
        select(h, 1)
        select(h, 3)
        dispatch(h, 0)
    for dz in range(8):
        dense["a2", dz].wait_recv()
        dense["b2", dz].wait_recv()
    for h in (0, 1):
        select(h, 2)
        dispatch(h, 1)

    for load in loads:
        load.wait()
    acc[...] = jnp.zeros_like(acc)
    for d in (0, 1, 3, 2):
        for dc in (0, 1):
            k = (core + dc) % 2
            for h in (0, 1):
                index = d * 2 + dc
                for part in (0, 1):
                    if d == 0 and dc == 0:
                        kept[h, part].wait()
                    else:
                        moved[h, part, (4 - d) % 4, dc].wait_recv()
                term = jnp.dot(
                    got[h][index].reshape(192, 1024),
                    w_in[columns(k, h), :],
                    preferred_element_type=F32,
                ).reshape(4, 48, 768)
                if h == 0:
                    acc[:, SPOS[d]] += term
                else:
                    acc[SPOS[d]] += term
    for i in range(4):
        gate = acc[i, :, :, 0:384]
        hid[i] = (gate / (1.0 + jnp.exp(-gate)) * acc[i, :, :, 384:768]).astype(BF)

    returned = {}
    for d in (2, 1, 3, 0):
        for dc in (0, 1):
            k = (core + dc) % 2
            for h in (0, 1):
                rows_in = hid[:, SPOS[d]] if h == 0 else hid[SPOS[d]]
                block_out = (
                    jnp.dot(
                        rows_in.reshape(192, 384), w_out[:, columns(k, h)], preferred_element_type=F32
                    )
                    .astype(BF)
                    .reshape(4, 48, 1024)
                )
                if d == 0 and dc == 0:
                    back[h][:, 0] = block_out
                    continue
                index = d * 2 + dc
                target = ((4 - d) % 4) * 2 + dc
                got[h][index] = block_out
                for part in (1, 0):
                    span = pl.ds(0, 3) if part == 0 else pl.ds(3, 1)
                    returned[h, part, d, dc] = links.send(
                        got[h].at[index, span], back[h].at[span, target], toward(h, d, dc)
                    )

    def combine(h, d):
        info = metas(h, d)
        found = lax.dot_general(info, pick[h], NT, preferred_element_type=F32)
        scale = lax.dot_general(info, pick_w[h], NT, preferred_element_type=F32)
        spread_out = jnp.where(found == rank_mask_t[...], scale, 0.0).astype(BF)
        return jnp.dot(
            spread_out, back[h][SPOS[d]].reshape(384, 1024), preferred_element_type=F32
        )

    def line(h, d):
        return at(dy=d) if h else at(dx=d)

    halves = {}
    parts = {}
    for h in (0, 1):
        for d in (1, 2, 3, 0):
            for dc in (0, 1):
                if d or dc:
                    returned[h, 1, d, dc].wait_recv()
        half_send[h] = combine(h, 2).astype(BF)
        halves[h, 1] = links.send(
            half_send.at[h, pl.ds(0, 128)], half_recv.at[h, pl.ds(0, 128)], line(h, 1)
        )
        halves[h, 3] = links.send(
            half_send.at[h, pl.ds(128, 128)], half_recv.at[h, pl.ds(128, 128)], line(h, 3)
        )
    for h in (0, 1):
        for d in (1, 2, 3, 0):
            for dc in (0, 1):
                if d or dc:
                    returned[h, 0, d, dc].wait_recv()
        first = combine(h, 1)
        third = combine(h, 3)
        halves[h, 1].wait_recv()
        part_send[h, 0, 0:128] = (first[0:128] + half_recv[h, 0:128].astype(F32)).astype(BF)
        part_send[h, 0, 128:256] = first[128:256].astype(BF)
        parts[h, 1] = links.send(part_send.at[h, 0], part_recv.at[h, 0], line(h, 1))
        halves[h, 3].wait_recv()
        part_send[h, 1, 0:128] = third[0:128].astype(BF)
        part_send[h, 1, 128:256] = (third[128:256] + half_recv[h, 128:256].astype(F32)).astype(BF)
        parts[h, 3] = links.send(part_send.at[h, 1], part_recv.at[h, 1], line(h, 3))
    for h in (0, 1):
        total[:, h * 1024 : (h + 1) * 1024] = combine(h, 0)
    for h in (0, 1):
        parts[h, 1].wait_recv()
        parts[h, 3].wait_recv()
        total[:, h * 1024 : (h + 1) * 1024] += part_recv[h, 0].astype(F32) + part_recv[
            h, 1
        ].astype(F32)

    z_send[4] = total[128:160].astype(BF)
    up = links.send(z_send.at[4, pl.ds(0, 16)], z_plus.at[3, pl.ds(0, 16)], z_up)
    down = links.send(z_send.at[4, pl.ds(16, 16)], z_minus.at[3, pl.ds(16, 16)], z_down)
    for i in (3, 2, 1):
        rest = 8 - i
        up.wait_recv()
        if i == 3:
            z_send[i, 0:16] = (total[96:112] + z_plus[3, 0:16].astype(F32)).astype(BF)
            z_send[i, 16:32] = total[112:128].astype(BF)
        else:
            z_send[i] = (total[i * 32 : i * 32 + 32] + z_plus[i].astype(F32)).astype(BF)
        up = links.send(z_send.at[i], z_plus.at[i - 1], z_up)
        down.wait_recv()
        if i == 3:
            z_send[rest, 0:16] = total[160:176].astype(BF)
            z_send[rest, 16:32] = (total[176:192] + z_minus[3, 16:32].astype(F32)).astype(BF)
        else:
            z_send[rest] = (
                total[rest * 32 : rest * 32 + 32] + z_minus[i].astype(F32)
            ).astype(BF)
        down = links.send(z_send.at[rest], z_minus.at[i - 1], z_down)
    up.wait_recv()
    down.wait_recv()
    total[0:32] += z_plus[0].astype(F32) + z_minus[0].astype(F32)

    other_rows = pl.ds(pl.multiple_of(other * 16, 16), 16)
    core_send[...] = total[other_rows, :]
    swap = links.send(core_send, core_recv, sibling)
    out[:, pl.ds(pl.multiple_of(core * 2048, 2048), 2048)] = total[own_rows, :]
    swap.wait_recv()
    out[:, pl.ds(pl.multiple_of(other * 2048, 2048), 2048)] = core_recv[...]
    links.finish()


def moe(normed, ids, gates, w_gate, w_up, w_down):
    vmem = pl.BlockSpec(memory_space=pltpu.VMEM)
    hbm = pl.BlockSpec(memory_space=pl.ANY)
    return pl.pallas_call(
        moe_kernel,
        out_shape=jax.ShapeDtypeStruct((16, D), F32),
        in_specs=[vmem, vmem, vmem, hbm, hbm, hbm],
        out_specs=vmem,
        scratch_shapes=[
            pltpu.VMEM((256, 2176), BF),
            pltpu.VMEM((16, 2176), BF),
            pltpu.VMEM((4, 256, 1152), BF),
            pltpu.VMEM((4, 256, 1152), BF),
            pltpu.VMEM((4, 8, 48, 1024), BF),
            pltpu.VMEM((4, 8, 48, 1024), BF),
            pltpu.VMEM((8, 4, 48, 1024), BF),
            pltpu.VMEM((8, 4, 48, 1024), BF),
            pltpu.VMEM((4, 8, 48, 1024), BF),
            pltpu.VMEM((4, 8, 48, 1024), BF),
            pltpu.VMEM((4, 4, 48, 768), F32),
            pltpu.VMEM((4, 4, 48, 384), BF),
            pltpu.VMEM((4096, 768), BF),
            pltpu.VMEM((384, 4096), BF),
            pltpu.VMEM((384, 256), F32),
            pltpu.VMEM((256, 384), F32),
            pltpu.VMEM((2, 256, 1024), BF),
            pltpu.VMEM((2, 256, 1024), BF),
            pltpu.VMEM((2, 2, 256, 1024), BF),
            pltpu.VMEM((2, 2, 256, 1024), BF),
            pltpu.VMEM((256, 2048), F32),
            pltpu.VMEM((8, 32, 2048), BF),
            pltpu.VMEM((4, 32, 2048), BF),
            pltpu.VMEM((4, 32, 2048), BF),
            pltpu.VMEM((16, 2048), F32),
            pltpu.VMEM((16, 2048), F32),
            pltpu.SemaphoreType.DMA((MOE_SEMS,)),
            pltpu.SemaphoreType.DMA((MOE_SEMS,)),
            pltpu.SemaphoreType.DMA((8,)),
        ],
        compiler_params=pltpu.CompilerParams(
            collective_id=1, has_side_effects=True, vmem_limit_bytes=58 * 2**20
        ),
        name="moe",
    )(normed, ids, gates, w_gate, w_up, w_down)


def shards(
    queries,
    keys,
    values,
    prefix_keys,
    prefix_values,
    out_weight,
    residual_in,
    norm_gain,
    expert_ids,
    route_weights,
    w_gate,
    w_up,
    w_down,
):
    seq_count = lax.axis_size("seq")
    expert_count = lax.axis_size("expert")
    seq_place = lax.axis_index("seq")
    expert_place = lax.axis_index("expert")
    block_len, seq_num, query_width = queries.shape
    heads_local = query_width // HD
    head_group = heads_local * expert_count // KV
    shared_head = expert_place * heads_local // head_group
    own_keys = lax.dynamic_slice_in_dim(keys, shared_head * HD, HD, 2)
    own_values = lax.dynamic_slice_in_dim(values, shared_head * HD, HD, 2)
    prefix_key = lax.dynamic_slice_in_dim(prefix_keys, shared_head * HD, HD, 1)
    prefix_value = lax.dynamic_slice_in_dim(prefix_values, shared_head * HD, HD, 1)
    score_scale = 1.0 / math.sqrt(HD)
    grouped_q = queries.reshape(block_len, seq_num, heads_local, HD)
    prefix_scores = (
        jnp.einsum("ibhd,pd->bhip", grouped_q, prefix_key, preferred_element_type=jnp.float32)
        * score_scale
    )
    prefix_top = jnp.max(prefix_scores, -1)
    prefix_weights = jnp.exp(prefix_scores - prefix_top[..., None]).astype(jnp.bfloat16)
    prefix_total = jnp.sum(prefix_weights, -1, dtype=jnp.float32)
    prefix_sum = jnp.einsum(
        "bhip,pd->bhid", prefix_weights, prefix_value, preferred_element_type=jnp.float32
    )
    query_places = seq_place * block_len + jnp.arange(block_len, dtype=jnp.int32)
    row_top = prefix_top
    row_total = prefix_total
    weighted = prefix_sum
    piece_keys = lax.all_gather(own_keys, "seq", axis=0, tiled=True)
    piece_values = lax.all_gather(own_values, "seq", axis=0, tiled=True)
    key_count = piece_keys.shape[0]
    scores = (
        jnp.einsum("ibhd,jbd->bhij", grouped_q, piece_keys, preferred_element_type=jnp.float32)
        * score_scale
    )
    key_places = jnp.arange(key_count, dtype=jnp.int32)
    allowed = key_places[None, :] <= query_places[:, None]
    scores = jnp.where(allowed, scores, -1e30)
    new_top = jnp.maximum(row_top, jnp.max(scores, -1))
    probabilities = jnp.exp(scores - new_top[..., None]).astype(jnp.bfloat16)
    shrink = jnp.exp(row_top - new_top)
    row_total = row_total * shrink + jnp.sum(probabilities, -1, dtype=jnp.float32)
    weighted = weighted * shrink[..., None] + jnp.einsum(
        "bhij,jbd->bhid", probabilities, piece_values, preferred_element_type=jnp.float32
    )
    row_top, row_total, weighted = (new_top, row_total, weighted)
    attended = (weighted / row_total[..., None]).astype(jnp.bfloat16)
    attended = jnp.transpose(attended, (2, 0, 1, 3)).reshape(block_len * seq_num, heads_local * HD)
    term_rows = jnp.dot(
        attended,
        lax.all_gather(out_weight, "seq", axis=1, tiled=True),
        preferred_element_type=jnp.float32,
    )
    summed = lax.psum_scatter(
        term_rows.astype(jnp.bfloat16), "expert", scatter_dimension=0, tiled=True
    ).astype(jnp.float32)
    hidden_state = residual_in.reshape(-1, D).astype(jnp.float32) + summed
    square = jnp.mean(hidden_state * hidden_state, -1, keepdims=True)
    normed = (hidden_state * lax.rsqrt(square + 1e-06) * norm_gain.astype(jnp.float32)).astype(
        jnp.bfloat16
    )
    mixed = moe(
        normed,
        expert_ids.reshape(16, TOPK),
        route_weights.reshape(16, TOPK),
        w_gate[0, 0],
        w_up[0, 0],
        w_down[0, 0],
    )
    return (hidden_state + mixed).astype(jnp.bfloat16).reshape(residual_in.shape)


def solution(mesh):
    in_specs = (
        P("seq", None, "expert"),
        P("seq", None, None),
        P("seq", None, None),
        P(),
        P(),
        P("expert", "seq"),
        P(("seq", "expert"), None, None),
        P(),
        P(("seq", "expert"), None, None),
        P(("seq", "expert"), None, None),
        P("seq", "expert", None, None),
        P("seq", "expert", None, None),
        P("seq", "expert", None, None),
    )
    out_specs = P(("seq", "expert"), None, None)
    return jax.shard_map(shards, mesh=mesh, in_specs=in_specs, out_specs=out_specs, check_vma=False)
```

```python
import math

import jax
import jax.numpy as jnp
from jax import lax
from jax.experimental import pallas as pl
from jax.experimental.pallas import tpu as pltpu
from jax.sharding import PartitionSpec as P

D = 4096
HD = 128
TOPK = 8

MESH = pl.DeviceIdType.MESH
BF = jnp.bfloat16
F32 = jnp.float32
NT = (((1,), (1,)), ((), ()))
ORDER = (0, 1, 3, 2)
SPOS = {0: 0, 1: 1, 3: 2, 2: 3}
MOE_SEMS = 160


def place():
    s = lax.axis_index("seq")
    e = lax.axis_index("expert")
    return (e // 8) * 2 + s // 8, (e // 2) % 4, s % 8, e % 2


def device(x, y, z, c):
    return ((x % 2) * 8 + z, ((x // 2) * 4 + y) * 2 + c)


class Links:
    def __init__(self, send_sems, recv_sems):
        self.send_sems = send_sems
        self.recv_sems = recv_sems
        self.used = 0
        self.open = []

    def send(self, src, dst, peer):
        index = self.used
        self.used += 1
        copy = pltpu.make_async_remote_copy(
            src_ref=src,
            dst_ref=dst,
            send_sem=self.send_sems.at[index],
            recv_sem=self.recv_sems.at[index],
            device_id=peer,
            device_id_type=MESH,
        )
        copy.start()
        self.open.append(copy)
        return copy

    def finish(self):
        for copy in self.open:
            copy.wait_send()
        self.open = []


def greet(peers):
    barrier = pltpu.get_barrier_semaphore()
    for peer in peers:
        pl.semaphore_signal(barrier, inc=1, device_id=peer, device_id_type=MESH)
    return lambda: pl.semaphore_wait(barrier, len(peers))


def moe_kernel(
    normed,
    ids,
    gates,
    w_gate,
    w_up,
    w_down,
    out,
    tok,
    stage,
    tok_a,
    tok_b,
    slot_a,
    slot_b,
    got_a,
    got_b,
    back_a,
    back_b,
    acc,
    hid,
    w_in,
    w_out,
    rank_mask,
    rank_mask_t,
    half_send,
    half_recv,
    part_send,
    part_recv,
    total,
    z_send,
    z_plus,
    z_minus,
    core_send,
    core_recv,
    send_sems,
    recv_sems,
    local_sems,
):
    x, y, z, core = place()
    other = 1 - core

    def at(dx=0, dy=0, dz=0, dc=0):
        return device((x + dx) % 4, (y + dy) % 4, (z + dz) % 8, (core + dc) % 2)

    sibling = at(dc=1)
    peers = [sibling, at(dz=1), at(dz=7)]
    for d in (1, 2, 3):
        for dc in (0, 1):
            peers.append(at(dx=d, dc=dc))
            peers.append(at(dy=d, dc=dc))
    arrived = greet(peers)
    loads = [
        pltpu.make_async_copy(w_gate, w_in.at[:, 0:384], local_sems.at[0]),
        pltpu.make_async_copy(w_up, w_in.at[:, 384:768], local_sems.at[1]),
        pltpu.make_async_copy(w_down, w_out, local_sems.at[2]),
    ]
    for load in loads:
        load.start()

    lane = lax.broadcasted_iota(jnp.int32, (16, 128), 1)
    chosen = jnp.zeros((16, 128), F32)
    weight = jnp.zeros((16, 128), F32)
    for j in range(TOPK):
        column = ids[:, j : j + 1]
        chosen = chosen + jnp.where(lane == column, 1.0, 0.0)
        weight = weight + jnp.where(lane == column + 64, gates[:, j : j + 1], 0.0)
    row_i = lax.broadcasted_iota(jnp.int32, (16, 16), 0)
    col_i = lax.broadcasted_iota(jnp.int32, (16, 16), 1)
    lower = jnp.where(col_i <= row_i, 1.0, 0.0).astype(BF)
    rank = jnp.dot(lower, chosen.astype(BF), preferred_element_type=F32)
    meta = (rank * chosen + weight).astype(BF)

    own_rows = pl.ds(pl.multiple_of(core * 16, 16), 16)

    def columns(k, h):
        return pl.ds(pl.multiple_of(k * 2048 + h * 1024, 1024), 1024)

    stage[:, 0:1024] = normed[:, columns(other, 0)]
    stage[:, 1024:1152] = meta
    stage[:, 1152:2176] = normed[:, columns(other, 1)]
    tok[own_rows, 0:1024] = normed[:, columns(core, 0)]
    tok[own_rows, 1024:1152] = meta
    tok[own_rows, 1152:2176] = normed[:, columns(core, 1)]

    links = Links(send_sems, recv_sems)
    arrived()
    links.send(stage, tok.at[own_rows], sibling).wait_recv()

    def rows(dz):
        return pl.ds(dz * 32, 32)

    dense = {}

    def spread(dz):
        r = rows(dz)
        dense["a3", dz] = links.send(tok.at[r, 0:1152], tok_a.at[3, r], at(dx=1))
        dense["b3", dz] = links.send(tok.at[r, 1024:2176], tok_b.at[3, r], at(dy=1))
        dense["a1", dz] = links.send(tok.at[r, 0:1152], tok_a.at[1, r], at(dx=3))
        dense["b1", dz] = links.send(tok.at[r, 1024:2176], tok_b.at[1, r], at(dy=3))

    def relay_up(dz):
        r = rows(dz)
        dense["a3", dz].wait_recv()
        dense["a2", dz] = links.send(tok_a.at[3, r], tok_a.at[2, r], at(dx=1))
        dense["b3", dz].wait_recv()
        dense["b2", dz] = links.send(tok_b.at[3, r], tok_b.at[2, r], at(dy=1))

    def relay_down(dz):
        r = rows(dz)
        dense["a1", dz].wait_recv()
        dense["a2", dz] = links.send(tok_a.at[1, r], tok_a.at[2, r], at(dx=3))
        dense["b1", dz].wait_recv()
        dense["b2", dz] = links.send(tok_b.at[1, r], tok_b.at[2, r], at(dy=3))

    z_up, z_down = at(dz=1), at(dz=7)
    up = links.send(tok.at[rows(0)], tok.at[rows(7)], z_up)
    down = links.send(tok.at[rows(0)], tok.at[rows(1)], z_down)
    spread(0)

    n = lax.broadcasted_iota(jnp.int32, (8, 48, 256), 1)
    t = lax.broadcasted_iota(jnp.int32, (8, 48, 256), 2)
    block = (n * 171) >> 9
    rank_mask[...] = (
        jnp.where(block == (t >> 4), n - 3 * block + 1, -1).astype(F32).reshape(384, 256)
    )
    r = lax.broadcasted_iota(jnp.int32, (256, 384), 1)
    t = lax.broadcasted_iota(jnp.int32, (256, 384), 0)
    n = r - 48 * ((r * 1366) >> 16)
    block = (n * 171) >> 9
    rank_mask_t[...] = jnp.where(block == (t >> 4), n - 3 * block + 1, -1).astype(F32)

    q = lax.broadcasted_iota(jnp.int32, (8, 48, 128), 0)
    lane = lax.broadcasted_iota(jnp.int32, (8, 48, 128), 2)
    step = q >> 1
    to_core = (core + (q & 1)) & 1
    to_y = (y + step) & 3
    to_x = (x + step) & 3
    half = z // 4
    expert_a = 4 * ((x // 2 * 4 + to_y) * 2 + to_core) + 2 * (x % 2) + half
    expert_b = 4 * (((to_x >> 1) * 4 + y) * 2 + to_core) + 2 * (to_x & 1) + half
    pick_a = jnp.where(lane == expert_a, 1.0, 0.0).astype(BF).reshape(384, 128)
    pick_b = jnp.where(lane == expert_b, 1.0, 0.0).astype(BF).reshape(384, 128)
    pick_aw = jnp.where(lane == expert_a + 64, 1.0, 0.0).astype(BF).reshape(384, 128)
    pick_bw = jnp.where(lane == expert_b + 64, 1.0, 0.0).astype(BF).reshape(384, 128)

    up.wait_recv()
    up = links.send(tok.at[rows(7)], tok.at[rows(6)], z_up)
    down.wait_recv()
    down = links.send(tok.at[rows(1)], tok.at[rows(2)], z_down)
    spread(7)
    spread(1)
    relay_up(0)
    up.wait_recv()
    up = links.send(tok.at[rows(6)], tok.at[rows(5)], z_up)
    down.wait_recv()
    down = links.send(tok.at[rows(2)], tok.at[rows(3)], z_down)
    spread(6)
    spread(2)
    relay_up(7)
    relay_down(1)
    up.wait_recv()
    up = links.send(tok.at[pl.ds(5 * 32, 16)], tok.at[pl.ds(4 * 32, 16)], z_up)
    down.wait_recv()
    down = links.send(tok.at[pl.ds(3 * 32 + 16, 16)], tok.at[pl.ds(4 * 32 + 16, 16)], z_down)
    spread(5)
    spread(3)
    relay_up(6)
    relay_down(2)
    up.wait_recv()
    down.wait_recv()
    spread(4)
    relay_up(5)
    relay_down(3)

    def tokens(h, d):
        if d == 0:
            return tok[:, 0:1024] if h == 0 else tok[:, 1152:2176]
        return tok_a[d, :, 0:1024] if h == 0 else tok_b[d, :, 128:1152]

    def metas(h, d):
        if d == 0:
            return tok[:, 1024:1152]
        return tok_a[d, :, 1024:1152] if h == 0 else tok_b[d, :, 0:128]

    slot = (slot_a, slot_b)
    got = (got_a, got_b)
    back = (back_a, back_b)
    pick = (pick_a, pick_b)
    pick_w = (pick_aw, pick_bw)

    def select(h, d):
        found = lax.dot_general(pick[h], metas(h, d), NT, preferred_element_type=F32)
        chosen = jnp.where(found == rank_mask[...], 1.0, 0.0).astype(BF)
        picked = jnp.dot(chosen, tokens(h, d), preferred_element_type=F32)
        slot[h][SPOS[d]] = picked.astype(BF).reshape(8, 48, 1024)

    def toward(h, d, dc):
        return at(dx=d, dc=dc) if h else at(dy=d, dc=dc)

    moved = {}
    kept = {}

    def dispatch(h, part):
        span = pl.ds(0, 3) if part == 0 else pl.ds(3, 1)
        for d in (2, 1, 3, 0):
            for dc in (0, 1):
                src = slot[h].at[span, d * 2 + dc]
                dst = got[h].at[((4 - d) % 4) * 2 + dc, span]
                if d == 0 and dc == 0:
                    copy = pltpu.make_async_copy(src, dst, local_sems.at[3 + h * 2 + part])
                    copy.start()
                    kept[h, part] = copy
                else:
                    moved[h, part, d, dc] = links.send(src, dst, toward(h, d, dc))

    select(0, 0)
    select(1, 0)
    for dz in range(8):
        if dz not in (0, 7, 6, 5):
            dense["a3", dz].wait_recv()
            dense["b3", dz].wait_recv()
        if dz not in (1, 2, 3, 4):
            dense["a1", dz].wait_recv()
            dense["b1", dz].wait_recv()
        if dz == 4:
            relay_down(4)
    for h in (0, 1):
        select(h, 1)
        select(h, 3)
        dispatch(h, 0)
    for dz in range(8):
        dense["a2", dz].wait_recv()
        dense["b2", dz].wait_recv()
    for h in (0, 1):
        select(h, 2)
        dispatch(h, 1)

    for load in loads:
        load.wait()
    acc[...] = jnp.zeros_like(acc)
    for d in (0, 1, 3, 2):
        for dc in (0, 1):
            k = (core + dc) % 2
            for h in (0, 1):
                index = d * 2 + dc
                for part in (0, 1):
                    if d == 0 and dc == 0:
                        kept[h, part].wait()
                    else:
                        moved[h, part, (4 - d) % 4, dc].wait_recv()
                term = jnp.dot(
                    got[h][index].reshape(192, 1024),
                    w_in[columns(k, h), :],
                    preferred_element_type=F32,
                ).reshape(4, 48, 768)
                if h == 0:
                    acc[:, SPOS[d]] += term
                else:
                    acc[SPOS[d]] += term
    for i in range(4):
        gate = acc[i, :, :, 0:384]
        hid[i] = (gate / (1.0 + jnp.exp(-gate)) * acc[i, :, :, 384:768]).astype(BF)

    returned = {}
    for d in (2, 1, 3, 0):
        for dc in (0, 1):
            k = (core + dc) % 2
            for h in (0, 1):
                rows_in = hid[:, SPOS[d]] if h == 0 else hid[SPOS[d]]
                block_out = (
                    jnp.dot(
                        rows_in.reshape(192, 384), w_out[:, columns(k, h)], preferred_element_type=F32
                    )
                    .astype(BF)
                    .reshape(4, 48, 1024)
                )
                if d == 0 and dc == 0:
                    back[h][:, 0] = block_out
                    continue
                index = d * 2 + dc
                target = ((4 - d) % 4) * 2 + dc
                got[h][index] = block_out
                for part in (1, 0):
                    span = pl.ds(0, 3) if part == 0 else pl.ds(3, 1)
                    returned[h, part, d, dc] = links.send(
                        got[h].at[index, span], back[h].at[span, target], toward(h, d, dc)
                    )

    def combine(h, d):
        info = metas(h, d)
        found = lax.dot_general(info, pick[h], NT, preferred_element_type=F32)
        scale = lax.dot_general(info, pick_w[h], NT, preferred_element_type=F32)
        spread_out = jnp.where(found == rank_mask_t[...], scale, 0.0).astype(BF)
        return jnp.dot(
            spread_out, back[h][SPOS[d]].reshape(384, 1024), preferred_element_type=F32
        )

    def line(h, d):
        return at(dy=d) if h else at(dx=d)

    halves = {}
    parts = {}
    for h in (0, 1):
        for d in (1, 2, 3, 0):
            for dc in (0, 1):
                if d or dc:
                    returned[h, 1, d, dc].wait_recv()
        half_send[h] = combine(h, 2).astype(BF)
        halves[h, 1] = links.send(
            half_send.at[h, pl.ds(0, 128)], half_recv.at[h, pl.ds(0, 128)], line(h, 1)
        )
        halves[h, 3] = links.send(
            half_send.at[h, pl.ds(128, 128)], half_recv.at[h, pl.ds(128, 128)], line(h, 3)
        )
    for h in (0, 1):
        for d in (1, 2, 3, 0):
            for dc in (0, 1):
                if d or dc:
                    returned[h, 0, d, dc].wait_recv()
        first = combine(h, 1)
        third = combine(h, 3)
        halves[h, 1].wait_recv()
        part_send[h, 0, 0:128] = (first[0:128] + half_recv[h, 0:128].astype(F32)).astype(BF)
        part_send[h, 0, 128:256] = first[128:256].astype(BF)
        parts[h, 1] = links.send(part_send.at[h, 0], part_recv.at[h, 0], line(h, 1))
        halves[h, 3].wait_recv()
        part_send[h, 1, 0:128] = third[0:128].astype(BF)
        part_send[h, 1, 128:256] = (third[128:256] + half_recv[h, 128:256].astype(F32)).astype(BF)
        parts[h, 3] = links.send(part_send.at[h, 1], part_recv.at[h, 1], line(h, 3))
    for h in (0, 1):
        total[:, h * 1024 : (h + 1) * 1024] = combine(h, 0)
    for h in (0, 1):
        parts[h, 1].wait_recv()
        parts[h, 3].wait_recv()
        total[:, h * 1024 : (h + 1) * 1024] += part_recv[h, 0].astype(F32) + part_recv[
            h, 1
        ].astype(F32)

    z_send[4] = total[128:160].astype(BF)
    up = links.send(z_send.at[4, pl.ds(0, 16)], z_plus.at[3, pl.ds(0, 16)], z_up)
    down = links.send(z_send.at[4, pl.ds(16, 16)], z_minus.at[3, pl.ds(16, 16)], z_down)
    for i in (3, 2, 1):
        rest = 8 - i
        up.wait_recv()
        if i == 3:
            z_send[i, 0:16] = (total[96:112] + z_plus[3, 0:16].astype(F32)).astype(BF)
            z_send[i, 16:32] = total[112:128].astype(BF)
        else:
            z_send[i] = (total[i * 32 : i * 32 + 32] + z_plus[i].astype(F32)).astype(BF)
        up = links.send(z_send.at[i], z_plus.at[i - 1], z_up)
        down.wait_recv()
        if i == 3:
            z_send[rest, 0:16] = total[160:176].astype(BF)
            z_send[rest, 16:32] = (total[176:192] + z_minus[3, 16:32].astype(F32)).astype(BF)
        else:
            z_send[rest] = (
                total[rest * 32 : rest * 32 + 32] + z_minus[i].astype(F32)
            ).astype(BF)
        down = links.send(z_send.at[rest], z_minus.at[i - 1], z_down)
    up.wait_recv()
    down.wait_recv()
    total[0:32] += z_plus[0].astype(F32) + z_minus[0].astype(F32)

    other_rows = pl.ds(pl.multiple_of(other * 16, 16), 16)
    core_send[...] = total[other_rows, :]
    swap = links.send(core_send, core_recv, sibling)
    out[:, pl.ds(pl.multiple_of(core * 2048, 2048), 2048)] = total[own_rows, :]
    swap.wait_recv()
    out[:, pl.ds(pl.multiple_of(other * 2048, 2048), 2048)] = core_recv[...]
    links.finish()


def moe(normed, ids, gates, w_gate, w_up, w_down):
    vmem = pl.BlockSpec(memory_space=pltpu.VMEM)
    hbm = pl.BlockSpec(memory_space=pl.ANY)
    return pl.pallas_call(
        moe_kernel,
        out_shape=jax.ShapeDtypeStruct((16, D), F32),
        in_specs=[vmem, vmem, vmem, hbm, hbm, hbm],
        out_specs=vmem,
        scratch_shapes=[
            pltpu.VMEM((256, 2176), BF),
            pltpu.VMEM((16, 2176), BF),
            pltpu.VMEM((4, 256, 1152), BF),
            pltpu.VMEM((4, 256, 1152), BF),
            pltpu.VMEM((4, 8, 48, 1024), BF),
            pltpu.VMEM((4, 8, 48, 1024), BF),
            pltpu.VMEM((8, 4, 48, 1024), BF),
            pltpu.VMEM((8, 4, 48, 1024), BF),
            pltpu.VMEM((4, 8, 48, 1024), BF),
            pltpu.VMEM((4, 8, 48, 1024), BF),
            pltpu.VMEM((4, 4, 48, 768), F32),
            pltpu.VMEM((4, 4, 48, 384), BF),
            pltpu.VMEM((4096, 768), BF),
            pltpu.VMEM((384, 4096), BF),
            pltpu.VMEM((384, 256), F32),
            pltpu.VMEM((256, 384), F32),
            pltpu.VMEM((2, 256, 1024), BF),
            pltpu.VMEM((2, 256, 1024), BF),
            pltpu.VMEM((2, 2, 256, 1024), BF),
            pltpu.VMEM((2, 2, 256, 1024), BF),
            pltpu.VMEM((256, 2048), F32),
            pltpu.VMEM((8, 32, 2048), BF),
            pltpu.VMEM((4, 32, 2048), BF),
            pltpu.VMEM((4, 32, 2048), BF),
            pltpu.VMEM((16, 2048), F32),
            pltpu.VMEM((16, 2048), F32),
            pltpu.SemaphoreType.DMA((MOE_SEMS,)),
            pltpu.SemaphoreType.DMA((MOE_SEMS,)),
            pltpu.SemaphoreType.DMA((8,)),
        ],
        compiler_params=pltpu.CompilerParams(
            collective_id=1, has_side_effects=True, vmem_limit_bytes=58 * 2**20
        ),
        name="moe",
    )(normed, ids, gates, w_gate, w_up, w_down)


ATT_SEMS = 96


def attn_kernel(
    queries,
    keys,
    values,
    prefix_keys,
    prefix_values,
    out_weight,
    residual,
    gain,
    hidden,
    normed,
    kv,
    wts,
    qs,
    pre_k,
    pre_v,
    scores,
    pre_scores,
    top,
    summed,
    weighted,
    att,
    att_bf,
    own_term,
    core_send,
    core_recv,
    y_send,
    y_recv,
    x_send,
    x_recv,
    send_sems,
    recv_sems,
    local_sems,
):
    x, y, z, core = place()
    other = 1 - core
    x_lo = x % 2
    kv_head = (lax.axis_index("expert")) // 4

    def at(dx=0, dy=0, dz=0, dc=0):
        return device((x + dx) % 4, (y + dy) % 4, (z + dz) % 8, (core + dc) % 2)

    sibling = at(dc=1)
    partner = device(x + 1 - 2 * x_lo, y, z, core)
    z_up, z_down = at(dz=1), at(dz=7)
    peers = [sibling, z_up, z_down]
    for d in (1, 2, 3):
        peers.append(at(dx=d))
        peers.append(at(dy=d))
    arrived = greet(peers)
    load = pltpu.make_async_copy(out_weight, wts.at[0], local_sems.at[0])
    load.start()
    for b in range(2):
        col = pl.ds(pl.multiple_of(b * 512 + kv_head * 128, 128), 128)
        kv[core, 0, :, b * 128 : (b + 1) * 128] = jnp.where(
            core == 0, keys[:, col].astype(F32), values[:, col].astype(F32)
        ).astype(BF)
    links = Links(send_sems, recv_sems)
    arrived()

    across = {}
    shared = {}

    def hand_on(dz):
        shared[0, dz] = links.send(kv.at[core, dz], kv.at[core, dz], sibling)
        across[dz] = links.send(kv.at[core, dz], kv.at[core, 8 + dz], partner)

    def hand_over(dz):
        across[dz].wait_recv()
        shared[1, dz] = links.send(kv.at[core, 8 + dz], kv.at[core, 8 + dz], sibling)

    low, high = pl.ds(0, 64), pl.ds(64, 64)
    up = links.send(kv.at[core, 0], kv.at[core, 7], z_up)
    down = links.send(kv.at[core, 0], kv.at[core, 1], z_down)
    hand_on(0)
    load.wait()
    w_up = links.send(wts.at[0], wts.at[7], z_up)
    w_down = links.send(wts.at[0], wts.at[1], z_down)

    for b in range(2):
        for h in range(4):
            qs[b, h * 128 : (h + 1) * 128, :] = queries[:, b * 512 + h * 128 : b * 512 + h * 128 + 128]
    head_cols = pl.ds(pl.multiple_of(kv_head * 128, 128), 128)
    pre_k[0:64] = prefix_keys[:, head_cols]
    pre_k[64:128] = jnp.zeros((64, 128), BF)
    pre_v[0:64] = prefix_values[:, head_cols]
    pre_v[64:128] = jnp.zeros((64, 128), BF)

    up.wait_recv()
    up = links.send(kv.at[core, 7], kv.at[core, 6], z_up)
    down.wait_recv()
    down = links.send(kv.at[core, 1], kv.at[core, 2], z_down)
    hand_on(7)
    hand_on(1)
    hand_over(0)
    up.wait_recv()
    up = links.send(kv.at[core, 6], kv.at[core, 5], z_up)
    down.wait_recv()
    down = links.send(kv.at[core, 2], kv.at[core, 3], z_down)
    hand_on(6)
    hand_on(2)
    hand_over(7)
    hand_over(1)
    up.wait_recv()
    up = links.send(kv.at[core, 5, low], kv.at[core, 4, low], z_up)
    down.wait_recv()
    down = links.send(kv.at[core, 3, high], kv.at[core, 4, high], z_down)
    hand_on(5)
    hand_on(3)
    hand_over(6)
    hand_over(2)
    up.wait_recv()
    down.wait_recv()
    hand_on(4)
    w_up.wait_recv()
    w_up = links.send(wts.at[7], wts.at[6], z_up)
    w_down.wait_recv()
    w_down = links.send(wts.at[1], wts.at[2], z_down)
    hand_over(5)
    hand_over(3)
    hand_over(4)
    for dz in range(8):
        shared[0, dz].wait_recv()
        shared[1, dz].wait_recv()

    scale = 1.0 / math.sqrt(HD)
    gap = lax.broadcasted_iota(jnp.int32, (4, 128, 128), 2) - lax.broadcasted_iota(
        jnp.int32, (4, 128, 128), 1
    )
    gap = gap.reshape(512, 128)
    pre_lane = lax.broadcasted_iota(jnp.int32, (512, 128), 1)

    def attend(b):
        cols = slice(b * 128, (b + 1) * 128)
        first = lax.dot_general(qs[b], pre_k[...], NT, preferred_element_type=F32) * scale
        first = jnp.where(pre_lane < 64, first, -1e30)
        pre_scores[...] = first
        top[...] = first

        def score(c, carry):
            block = lax.dot_general(
                qs[b],
                kv[0, pl.ds(2 * c, 2), :, cols].reshape(256, 128),
                NT,
                preferred_element_type=F32,
            )
            best = top[...]
            for r in range(2):
                theirs = ((x_lo + c // 4) % 2) * 8 + (z + 2 * c + r) % 8
                ahead = (x_lo * 8 + z - theirs) * 128
                part = jnp.where(gap <= ahead, block[:, r * 128 : (r + 1) * 128] * scale, -1e30)
                scores[c, :, r * 128 : (r + 1) * 128] = part
                best = jnp.maximum(best, part)
            top[...] = best
            return carry

        lax.fori_loop(0, 8, score, 0)
        top[...] = jnp.broadcast_to(jnp.max(top[...], -1, keepdims=True), (512, 128))
        probs = jnp.exp(pre_scores[...] - top[...]).astype(BF)
        summed[...] = probs.astype(F32)
        weighted[...] = jnp.dot(probs, pre_v[...], preferred_element_type=F32)

        def mix(c, carry):
            peak = top[...]
            left = jnp.exp(scores[c, :, 0:128] - peak).astype(BF)
            right = jnp.exp(scores[c, :, 128:256] - peak).astype(BF)
            summed[...] += left.astype(F32) + right.astype(F32)
            weighted[...] += jnp.dot(
                jnp.concatenate([left, right], axis=1),
                kv[1, pl.ds(2 * c, 2), :, cols].reshape(256, 128),
                preferred_element_type=F32,
            )
            return carry

        lax.fori_loop(0, 8, mix, 0)
        result = weighted[...] / jnp.sum(summed[...], -1, keepdims=True)
        for h in range(4):
            for e in range(16):
                start = h * 128 + e * 8
                att[e % 2, (e // 2) % 4, e // 8, b, :, h * 128 : (h + 1) * 128] = result[
                    start : start + 8
                ]

    attend(0)
    w_up.wait_recv()
    w_up = links.send(wts.at[6], wts.at[5], z_up)
    w_down.wait_recv()
    w_down = links.send(wts.at[2], wts.at[3], z_down)
    attend(1)
    att_bf[0] = att[...].reshape(256, 512).astype(BF)
    swap = links.send(att_bf.at[0], att_bf.at[1], partner)
    w_up.wait_recv()
    w_up = links.send(wts.at[5, pl.ds(0, 256)], wts.at[4, pl.ds(0, 256)], z_up)
    w_down.wait_recv()
    w_down = links.send(wts.at[3, pl.ds(256, 256)], wts.at[4, pl.ds(256, 256)], z_down)
    swap.wait_recv()

    def half(c):
        rows = pl.ds(pl.multiple_of(c * 128, 128), 128)
        return att_bf[:, rows, :].reshape(256, 512)

    chunks = ((0, 7), (1, 6), (2, 5), (3, 4))
    core_moves, y_moves, x_moves = {}, {}, {}

    def project(j):
        if j == 3:
            w_up.wait_recv()
            w_down.wait_recv()
        for i, dz in enumerate(chunks[j]):
            cols = slice(i * 256, (i + 1) * 256)
            core_send[j, :, :, :, :, cols] = (
                jnp.dot(half(other), wts[dz], preferred_element_type=F32)
                .astype(BF)
                .reshape(2, 4, 2, 16, 256)
            )
        core_moves[j] = links.send(core_send.at[j], core_recv.at[j], sibling)
        for i, dz in enumerate(chunks[j]):
            cols = slice(i * 256, (i + 1) * 256)
            own_term[j, :, :, :, :, cols] = jnp.dot(
                half(core), wts[dz], preferred_element_type=F32
            ).reshape(2, 4, 2, 16, 256)

    def along_y(j):
        core_moves[j].wait_recv()
        both = own_term[j] + core_recv[j].astype(F32)
        own_term[j] = both
        y_send[j] = both.astype(BF)
        for d in (2, 1, 3):
            y_moves[j, d] = links.send(
                y_send.at[j, :, (y + d) % 4], y_recv.at[j, (4 - d) % 4], at(dy=d)
            )

    def along_x(j):
        own = own_term[j, :, y]
        for d in (1, 2, 3):
            y_moves[j, d].wait_recv()
        for d in (1, 2, 3):
            own = own + y_recv[j, d].astype(F32)
        own_term[j, :, y] = own
        x_send[j] = own.astype(BF)
        for d in (2, 1, 3):
            x_moves[j, d] = links.send(
                x_send.at[j, d % 2, ((x + d) % 4) // 2], x_recv.at[j, (4 - d) % 4], at(dx=d)
            )

    square = jnp.zeros((16, 128), F32)

    def join(j, square):
        for d in (1, 2, 3):
            x_moves[j, d].wait_recv()
        mine = own_term[j, 0, y, x // 2] + x_recv[j, 2].astype(F32)
        theirs = x_recv[j, 1].astype(F32) + x_recv[j, 3].astype(F32)
        for i, dz in enumerate(chunks[j]):
            for side, part in ((x_lo, mine), (1 - x_lo, theirs)):
                where = pl.ds(pl.multiple_of((side * 8 + (z + dz) % 8) * 256, 256), 256)
                value = residual[:, where].astype(F32) + part[:, i * 256 : (i + 1) * 256]
                hidden[:, where] = value
                value = value * value
                square = square + value[:, 0:128] + value[:, 128:256]
        return square

    project(0)
    project(1)
    along_y(0)
    project(2)
    along_y(1)
    project(3)
    along_y(2)
    along_x(0)
    along_y(3)
    for j in (1, 2, 3):
        along_x(j)
    for j in range(4):
        square = join(j, square)
    mean = jnp.sum(square, -1, keepdims=True) * (1.0 / D)
    normed[...] = (hidden[...] * lax.rsqrt(mean + 1e-06) * gain[...].astype(F32)).astype(BF)
    links.finish()


def attention(queries, keys, values, prefix_keys, prefix_values, out_weight, residual, gain):
    vmem = pl.BlockSpec(memory_space=pltpu.VMEM)
    hbm = pl.BlockSpec(memory_space=pl.ANY)
    return pl.pallas_call(
        attn_kernel,
        out_shape=(jax.ShapeDtypeStruct((16, D), F32), jax.ShapeDtypeStruct((16, D), BF)),
        in_specs=[vmem, vmem, vmem, vmem, vmem, hbm, vmem, vmem],
        out_specs=(vmem, vmem),
        scratch_shapes=[
            pltpu.VMEM((2, 16, 128, 256), BF),
            pltpu.VMEM((8, 512, 256), BF),
            pltpu.VMEM((2, 512, 128), BF),
            pltpu.VMEM((128, 128), BF),
            pltpu.VMEM((128, 128), BF),
            pltpu.VMEM((8, 512, 256), F32),
            pltpu.VMEM((512, 128), F32),
            pltpu.VMEM((512, 128), F32),
            pltpu.VMEM((512, 128), F32),
            pltpu.VMEM((512, 128), F32),
            pltpu.VMEM((2, 4, 2, 2, 8, 512), F32),
            pltpu.VMEM((2, 256, 512), BF),
            pltpu.VMEM((4, 2, 4, 2, 16, 512), F32),
            pltpu.VMEM((4, 2, 4, 2, 16, 512), BF),
            pltpu.VMEM((4, 2, 4, 2, 16, 512), BF),
            pltpu.VMEM((4, 2, 4, 2, 16, 512), BF),
            pltpu.VMEM((4, 4, 2, 2, 16, 512), BF),
            pltpu.VMEM((4, 2, 2, 16, 512), BF),
            pltpu.VMEM((4, 4, 16, 512), BF),
            pltpu.SemaphoreType.DMA((ATT_SEMS,)),
            pltpu.SemaphoreType.DMA((ATT_SEMS,)),
            pltpu.SemaphoreType.DMA((1,)),
        ],
        compiler_params=pltpu.CompilerParams(
            collective_id=2, has_side_effects=True, vmem_limit_bytes=48 * 2**20
        ),
        name="attention",
    )(queries, keys, values, prefix_keys, prefix_values, out_weight, residual, gain)


def shards(
    queries,
    keys,
    values,
    prefix_keys,
    prefix_values,
    out_weight,
    residual_in,
    norm_gain,
    expert_ids,
    route_weights,
    w_gate,
    w_up,
    w_down,
):
    def by_sequence(array):
        return jnp.transpose(array, (1, 0, 2)).reshape(16, array.shape[-1])

    hidden_state, normed = attention(
        queries.reshape(128, 1024),
        keys.reshape(128, 1024),
        values.reshape(128, 1024),
        prefix_keys,
        prefix_values,
        out_weight,
        by_sequence(residual_in),
        norm_gain.reshape(1, D),
    )
    mixed = moe(
        normed,
        by_sequence(expert_ids),
        by_sequence(route_weights),
        w_gate[0, 0],
        w_up[0, 0],
        w_down[0, 0],
    )
    mixed = (hidden_state + mixed).astype(BF)
    return jnp.transpose(mixed.reshape(2, 8, D), (1, 0, 2))


def solution(mesh):
    in_specs = (
        P("seq", None, "expert"),
        P("seq", None, None),
        P("seq", None, None),
        P(),
        P(),
        P("expert", "seq"),
        P(("seq", "expert"), None, None),
        P(),
        P(("seq", "expert"), None, None),
        P(("seq", "expert"), None, None),
        P("seq", "expert", None, None),
        P("seq", "expert", None, None),
        P("seq", "expert", None, None),
    )
    out_specs = P(("seq", "expert"), None, None)
    return jax.shard_map(shards, mesh=mesh, in_specs=in_specs, out_specs=out_specs, check_vma=False)
```

```python
import math

import jax
import jax.numpy as jnp
from jax import lax
from jax.experimental import pallas as pl
from jax.experimental.pallas import tpu as pltpu
from jax.sharding import PartitionSpec as P

D = 4096
HD = 128
TOPK = 8

MESH = pl.DeviceIdType.MESH
BF = jnp.bfloat16
F32 = jnp.float32
NT = (((1,), (1,)), ((), ()))
ORDER = (0, 1, 3, 2)
SPOS = {0: 0, 1: 1, 3: 2, 2: 3}
MOE_SEMS = 104
FAR = (1, 2, 3)


def place():
    s = lax.axis_index("seq")
    e = lax.axis_index("expert")
    return (e // 8) * 2 + s // 8, (e // 2) % 4, s % 8, e % 2


def device(x, y, z, c):
    return ((x % 2) * 8 + z, ((x // 2) * 4 + y) * 2 + c)


class Links:
    def __init__(self, send_sems, recv_sems):
        self.send_sems = send_sems
        self.recv_sems = recv_sems
        self.used = 0
        self.open = []

    def copy(self, src, dst, peer, index):
        return pltpu.make_async_remote_copy(
            src_ref=src,
            dst_ref=dst,
            send_sem=self.send_sems.at[index],
            recv_sem=self.recv_sems.at[index],
            device_id=peer,
            device_id_type=MESH,
        )

    def send(self, src, dst, peer):
        copy = self.copy(src, dst, peer, self.used)
        self.used += 1
        copy.start()
        self.open.append(copy)
        return copy

    def send_group(self, copies, all_src, all_dst, peer=None):
        index = self.used
        self.used += 1
        for src, dst, to in copies:
            self.copy(src, dst, to, index).start()
        group = self.copy(all_src, all_dst, peer or copies[0][2], index)
        self.open.append(group)
        return group

    def more(self, index, src, dst, peer):
        self.copy(src, dst, peer, index).start()

    def finish(self):
        for copy in self.open:
            copy.wait_send()
        self.open = []


def greet(peers):
    barrier = pltpu.get_barrier_semaphore()
    for peer in peers:
        pl.semaphore_signal(barrier, inc=1, device_id=peer, device_id_type=MESH)
    return lambda: pl.semaphore_wait(barrier, len(peers))


def moe_kernel(
    normed,
    meta_a,
    meta_b,
    hidden,
    w_gate,
    w_up,
    w_down,
    out,
    mix,
    tok,
    stage,
    near,
    far,
    far_stage,
    slot,
    got,
    back,
    acc,
    hid,
    w_in,
    w_out,
    rank_mask,
    rank_mask_t,
    choose,
    scatter,
    part_send,
    part_recv,
    total,
    z_send,
    z_recv,
    far_total,
    far_send,
    far_plus,
    far_minus,
    line_send,
    line_recv,
    core_send,
    core_recv,
    send_sems,
    recv_sems,
    local_sems,
):
    x, y, z, core = place()
    other = 1 - core

    def at(dx=0, dy=0, dz=0, dc=0):
        return device((x + dx) % 4, (y + dy) % 4, (z + dz) % 8, (core + dc) % 2)

    def line(h, d):
        return at(dy=d) if h else at(dx=d)

    def toward(h, d, dc):
        return at(dx=d, dc=dc) if h else at(dy=d, dc=dc)

    sibling = at(dc=1)
    z_up, z_down = at(dz=1), at(dz=7)
    peers = [sibling] + [at(dz=d) for d in range(1, 8)]
    for d in (1, 2, 3):
        for dc in (0, 1):
            peers.append(at(dx=d, dc=dc))
            peers.append(at(dy=d, dc=dc))
    arrived = greet(peers)
    loads = [
        pltpu.make_async_copy(w_gate, w_in.at[:, 0:384], local_sems.at[0]),
        pltpu.make_async_copy(w_up, w_in.at[:, 384:768], local_sems.at[1]),
        pltpu.make_async_copy(w_down, w_out, local_sems.at[2]),
    ]
    for load in loads:
        load.start()

    def columns(k, h, c):
        return pl.ds(pl.multiple_of(k * 2048 + h * 1024 + c * 256, 256), 256)

    own_rows = pl.ds(pl.multiple_of(core * 16, 16), 16)
    for h in (0, 1):
        cols = slice(h * 256, (h + 1) * 256)
        stage[:, cols] = normed[:, columns(other, h, 0)]
        tok[own_rows, cols] = normed[:, columns(core, h, 0)]
        for c in FAR:
            far_stage[c - 1, h] = normed[:, columns(other, h, c)]
            far[c - 1, h, 0, 0, own_rows] = normed[:, columns(core, h, c)]

    links = Links(send_sems, recv_sems)
    arrived()
    swap = links.send(stage, tok.at[own_rows], sibling)
    far_swap = links.send(far_stage, far.at[:, :, 0, 0, own_rows], sibling)
    swap.wait_recv()

    def rows(dz):
        return pl.ds(dz * 32, 32)

    dense = {}

    def spread(dz):
        r = rows(dz)
        dense[dz] = links.send_group(
            [
                (tok.at[r, h * 256 : (h + 1) * 256], near.at[h, 4 - d, r], line(h, d))
                for d in (2, 1, 3)
                for h in (0, 1)
            ],
            near.at[:, 1:4, r],
            near.at[:, 1:4, r],
        )

    ring = {}
    for d in (1, 7, 2, 6, 3, 5, 4):
        ring[8 - d] = links.send(tok.at[rows(0)], tok.at[rows(8 - d)], at(dz=d))
    spread(0)
    far_swap.wait_recv()
    far_line = links.send_group(
        [
            (far.at[:, h, 0, 0], far.at[:, h, 0, 4 - d], line(h, d))
            for d in (2, 1, 3)
            for h in (0, 1)
        ],
        far.at[:, :, 0, 1:4],
        far.at[:, :, 0, 1:4],
    )

    n = lax.broadcasted_iota(jnp.int32, (8, 48, 256), 1)
    t = lax.broadcasted_iota(jnp.int32, (8, 48, 256), 2)
    block = (n * 171) >> 9
    rank_mask[...] = (
        jnp.where(block == (t >> 4), n - 3 * block + 1, -1).astype(F32).reshape(384, 256)
    )
    r = lax.broadcasted_iota(jnp.int32, (256, 384), 1)
    t = lax.broadcasted_iota(jnp.int32, (256, 384), 0)
    n = r - 48 * ((r * 1366) >> 16)
    block = (n * 171) >> 9
    rank_mask_t[...] = jnp.where(block == (t >> 4), n - 3 * block + 1, -1).astype(F32)
    q = lax.broadcasted_iota(jnp.int32, (8, 48, 128), 0)
    lane = lax.broadcasted_iota(jnp.int32, (8, 48, 128), 2)
    step = q >> 1
    to_core = (core + (q & 1)) & 1
    to_y = (y + step) & 3
    to_x = (x + step) & 3
    half = z // 4
    expert_a = 4 * ((x // 2 * 4 + to_y) * 2 + to_core) + 2 * (x % 2) + half
    expert_b = 4 * (((to_x >> 1) * 4 + y) * 2 + to_core) + 2 * (to_x & 1) + half
    metas = (meta_a, meta_b)

    def one_hot(match):
        return jnp.where(match, 1.0, 0.0).astype(BF).reshape(384, 128)

    def masks(h, d):
        expert = expert_b if h else expert_a
        pick = one_hot(lane == expert)
        info = metas[h][d]
        found = lax.dot_general(pick, info, NT, preferred_element_type=F32)
        choose[h, d] = jnp.where(found == rank_mask[...], 1.0, 0.0).astype(BF)
        found = lax.dot_general(info, pick, NT, preferred_element_type=F32)
        scale = lax.dot_general(info, one_hot(lane == expert + 64), NT, preferred_element_type=F32)
        scatter[h, d] = jnp.where(found == rank_mask_t[...], scale, 0.0).astype(BF)

    far_up, far_down = {}, {}

    def far_start(c):
        piece = far.at[c - 1]
        far_up[c] = links.send(piece.at[:, 0], piece.at[:, 7], z_up)
        far_down[c] = links.send(piece.at[:, 0], piece.at[:, 1], z_down)

    def far_step(c, i):
        piece = far.at[c - 1]
        far_up[c].wait_recv()
        far_down[c].wait_recv()
        if i < 3:
            far_up[c] = links.send(piece.at[:, 8 - i], piece.at[:, 7 - i], z_up)
            far_down[c] = links.send(piece.at[:, i], piece.at[:, i + 1], z_down)
        elif i == 3:
            left, right = pl.ds(0, 2), pl.ds(2, 2)
            far_up[c] = links.send(piece.at[:, 5, left], piece.at[:, 4, left], z_up)
            far_down[c] = links.send(piece.at[:, 3, right], piece.at[:, 4, right], z_down)

    for dz in (7, 1):
        ring[dz].wait_recv()
        spread(dz)
    far_line.wait_recv()
    far_start(1)
    masks(0, 0)
    for dz in (6, 2):
        ring[dz].wait_recv()
        spread(dz)
    masks(1, 0)
    for dz in (5, 3):
        ring[dz].wait_recv()
        spread(dz)
    masks(0, 1)
    ring[4].wait_recv()
    spread(4)
    far_start(2)
    masks(1, 1)
    masks(0, 3)
    far_step(1, 1)
    masks(1, 3)
    masks(0, 2)
    masks(1, 2)
    acc[...] = jnp.zeros_like(acc)

    def select(c, h, d):
        if c:
            tokens = far[c - 1, h, :, d].reshape(256, 256)
        elif d == 0:
            tokens = tok[:, h * 256 : (h + 1) * 256]
        else:
            tokens = near[h, d]
        picked = jnp.dot(choose[h, d], tokens, preferred_element_type=F32)
        slot[c, h, SPOS[d]] = picked.astype(BF).reshape(8, 48, 256)

    moved, kept = {}, {}

    def dispatch(c, h):
        for d in (0, 1, 3, 2):
            select(c, h, d)
        copies = []
        for d in (2, 1, 3, 0):
            for dc in (0, 1):
                src = slot.at[c, h, :, d * 2 + dc]
                dst = got.at[c, h, ((4 - d) % 4) * 2 + dc]
                if d == 0 and dc == 0:
                    kept[c, h] = pltpu.make_async_copy(src, dst, local_sems.at[3 + c * 2 + h])
                    kept[c, h].start()
                else:
                    copies.append((src, dst, toward(h, d, dc)))
        moved[c, h] = links.send_group(copies, slot.at[c, h, :, 1:8], got.at[c, h, 1:8])

    def expert_in(c, h):
        kept[c, h].wait()
        moved[c, h].wait_recv()
        for d in (0, 1, 3, 2):
            term = 0
            for dc in (0, 1):
                k = (core + dc) % 2
                term = term + jnp.dot(
                    got[c, h, d * 2 + dc].reshape(192, 256),
                    w_in[columns(k, h, c), :],
                    preferred_element_type=F32,
                )
            if h == 0:
                acc[:, SPOS[d]] += term.reshape(4, 48, 768)
            else:
                acc[SPOS[d]] += term.reshape(4, 48, 768)

    for dz in range(8):
        dense[dz].wait_recv()
    dispatch(0, 0)
    far_step(1, 2)
    dispatch(0, 1)
    far_step(2, 1)
    far_step(1, 3)
    far_start(3)
    for load in loads:
        load.wait()
    far_step(2, 2)
    far_step(1, 4)
    dispatch(1, 0)
    far_step(2, 3)
    far_step(3, 1)
    dispatch(1, 1)
    expert_in(0, 0)
    far_step(2, 4)
    far_step(3, 2)
    dispatch(2, 0)
    dispatch(2, 1)
    far_step(3, 3)
    expert_in(0, 1)
    far_step(3, 4)
    dispatch(3, 0)
    dispatch(3, 1)
    for c in FAR:
        for h in (0, 1):
            expert_in(c, h)
    for i in range(4):
        gate = acc[i, :, :, 0:384]
        hid[i] = (gate / (1.0 + jnp.exp(-gate)) * acc[i, :, :, 384:768]).astype(BF)

    returned = {}

    def expert_out(c, h):
        index = links.used
        returned[c, h] = links.send_group(
            [], got.at[c, h, 1:8], back.at[c, h, :, 1:8], sibling
        )
        for d in (2, 1, 3, 0):
            rows_in = hid[:, SPOS[d]] if h == 0 else hid[SPOS[d]]
            for dc in (0, 1):
                k = (core + dc) % 2
                block_out = (
                    jnp.dot(
                        rows_in.reshape(192, 384),
                        w_out[:, columns(k, h, c)],
                        preferred_element_type=F32,
                    )
                    .astype(BF)
                    .reshape(4, 48, 256)
                )
                if d == 0 and dc == 0:
                    back[c, h, :, 0] = block_out
                    continue
                target = ((4 - d) % 4) * 2 + dc
                got[c, h, d * 2 + dc] = block_out
                links.more(
                    index, got.at[c, h, d * 2 + dc], back.at[c, h, :, target], toward(h, d, dc)
                )

    def combine(c, h, d):
        return jnp.dot(
            scatter[h, d], back[c, h, SPOS[d]].reshape(384, 256), preferred_element_type=F32
        )

    def all_back(c, h):
        returned[c, h].wait_recv()

    def far_open(c):
        for h in (0, 1):
            all_back(c, h)
            for d in range(4):
                far_total[c - 1, h, d] = combine(c, h, d)
        send, left, right = far_send.at[c - 1], pl.ds(0, 2), pl.ds(2, 2)
        send[:, 4] = far_total[c - 1, :, :, 128:160].astype(BF)
        far_up[c] = links.send(send.at[:, 4, left], far_plus.at[c - 1, 3, :, left], z_up)
        far_down[c] = links.send(send.at[:, 4, right], far_minus.at[c - 1, 3, :, right], z_down)

    def far_return(c, i):
        rest = 8 - i
        left, right = slice(0, 2), slice(2, 4)
        send, plus, minus = far_send.at[c - 1], far_plus.at[c - 1], far_minus.at[c - 1]

        def mine(dz, span=slice(0, 4)):
            return far_total[c - 1, :, span, dz * 32 : dz * 32 + 32]

        far_up[c].wait_recv()
        if i == 3:
            send[:, i, left] = (mine(i, left) + plus[i, :, left].astype(F32)).astype(BF)
            send[:, i, right] = mine(i, right).astype(BF)
        else:
            send[:, i] = (mine(i) + plus[i].astype(F32)).astype(BF)
        far_up[c] = links.send(send.at[:, i], plus.at[i - 1], z_up)
        far_down[c].wait_recv()
        if i == 3:
            send[:, rest, left] = mine(rest, left).astype(BF)
            send[:, rest, right] = (mine(rest, right) + minus[i, :, right].astype(F32)).astype(BF)
        else:
            send[:, rest] = (mine(rest) + minus[i].astype(F32)).astype(BF)
        far_down[c] = links.send(send.at[:, rest], minus.at[i - 1], z_down)

    line_moves = {}

    def far_finish(c):
        far_up[c].wait_recv()
        far_down[c].wait_recv()
        ends = (
            far_total[c - 1, :, :, 0:32]
            + far_plus[c - 1, 0].astype(F32)
            + far_minus[c - 1, 0].astype(F32)
        )
        line_send[c - 1] = ends.astype(BF)
        line_moves[c] = links.send_group(
            [
                (line_send.at[c - 1, h, d], line_recv.at[c - 1, h, (4 - d) % 4], line(h, d))
                for d in (2, 1, 3)
                for h in (0, 1)
            ],
            line_send.at[c - 1, :, 1:4],
            line_recv.at[c - 1, :, 1:4],
        )
        far_total[c - 1, :, 0, 0:32] = ends[:, 0]

    def far_join(c):
        line_moves[c].wait_recv()
        for d in (1, 2, 3):
            far_total[c - 1, :, 0, 0:32] += line_recv[c - 1, :, d].astype(F32)

    parts = {}

    def near_part(h):
        all_back(0, h)
        for d in (2, 1, 3):
            part_send[h, d] = combine(0, h, d).astype(BF)
        parts[h] = links.send_group(
            [(part_send.at[h, d], part_recv.at[h, 4 - d], line(h, d)) for d in (2, 1, 3)],
            part_send.at[h, 1:4],
            part_recv.at[h, 1:4],
        )
        total[:, h * 256 : (h + 1) * 256] = combine(0, h, 0)

    def near_join(h):
        parts[h].wait_recv()
        rest = part_recv[h, 1].astype(F32) + part_recv[h, 2].astype(F32)
        total[:, h * 256 : (h + 1) * 256] += rest + part_recv[h, 3].astype(F32)

    def z_return():
        z_send[...] = total[...].reshape(8, 32, 512).astype(BF)
        return links.send_group(
            [(z_send.at[d], z_recv.at[8 - d], at(dz=d)) for d in (4, 3, 5, 2, 6, 1, 7)],
            z_send.at[1:8],
            z_recv.at[1:8],
        )

    for c in (1, 2):
        for h in (0, 1):
            expert_out(c, h)
    far_open(1)
    expert_out(3, 0)
    far_return(1, 3)
    expert_out(3, 1)
    far_return(1, 2)
    far_open(2)
    far_return(1, 1)
    expert_out(0, 0)
    far_return(2, 3)
    expert_out(0, 1)
    far_finish(1)
    far_return(2, 2)
    far_open(3)
    far_return(2, 1)
    far_return(3, 3)
    near_part(0)
    near_part(1)
    far_return(3, 2)
    far_finish(2)
    far_return(3, 1)
    near_join(0)
    near_join(1)
    ending = z_return()
    far_join(1)
    far_join(2)
    far_finish(3)
    far_join(3)
    other_rows = pl.ds(pl.multiple_of(other * 16, 16), 16)
    for h in (0, 1):
        for c in FAR:
            core_send[:, h * 1024 + c * 256 : h * 1024 + (c + 1) * 256] = far_total[
                c - 1, h, 0, other_rows
            ]
            mix[:, columns(core, h, c)] = far_total[c - 1, h, 0, own_rows]
    ending.wait_recv()
    ends = total[0:32]
    for d in range(1, 8):
        ends = ends + z_recv[d].astype(F32)
    total[0:32] = ends
    for h in (0, 1):
        core_send[:, h * 1024 : h * 1024 + 256] = total[other_rows, h * 256 : (h + 1) * 256]
    swap = links.send(core_send, core_recv, sibling)
    for h in (0, 1):
        mix[:, columns(core, h, 0)] = total[own_rows, h * 256 : (h + 1) * 256]
    swap.wait_recv()
    mix[:, pl.ds(pl.multiple_of(other * 2048, 2048), 2048)] = core_recv[...]
    result = hidden[...] + mix[...]
    out[...] = jnp.stack([result[0:8], result[8:16]], axis=1).astype(BF)
    links.finish()


def moe(*operands):
    vmem = pl.BlockSpec(memory_space=pltpu.VMEM)
    hbm = pl.BlockSpec(memory_space=pl.ANY)
    return pl.pallas_call(
        moe_kernel,
        out_shape=jax.ShapeDtypeStruct((8, 2, D), BF),
        in_specs=[vmem, vmem, vmem, vmem, hbm, hbm, hbm],
        out_specs=vmem,
        scratch_shapes=[
            pltpu.VMEM((16, D), F32),
            pltpu.VMEM((256, 512), BF),
            pltpu.VMEM((16, 512), BF),
            pltpu.VMEM((2, 4, 256, 256), BF),
            pltpu.VMEM((3, 2, 8, 4, 32, 256), BF),
            pltpu.VMEM((3, 2, 16, 256), BF),
            pltpu.VMEM((4, 2, 4, 8, 48, 256), BF),
            pltpu.VMEM((4, 2, 8, 4, 48, 256), BF),
            pltpu.VMEM((4, 2, 4, 8, 48, 256), BF),
            pltpu.VMEM((4, 4, 48, 768), F32),
            pltpu.VMEM((4, 4, 48, 384), BF),
            pltpu.VMEM((4096, 768), BF),
            pltpu.VMEM((384, 4096), BF),
            pltpu.VMEM((384, 256), F32),
            pltpu.VMEM((256, 384), F32),
            pltpu.VMEM((2, 4, 384, 256), BF),
            pltpu.VMEM((2, 4, 256, 384), BF),
            pltpu.VMEM((2, 4, 256, 256), BF),
            pltpu.VMEM((2, 4, 256, 256), BF),
            pltpu.VMEM((256, 512), F32),
            pltpu.VMEM((8, 32, 512), BF),
            pltpu.VMEM((8, 32, 512), BF),
            pltpu.VMEM((3, 2, 4, 256, 256), F32),
            pltpu.VMEM((3, 2, 8, 4, 32, 256), BF),
            pltpu.VMEM((3, 4, 2, 4, 32, 256), BF),
            pltpu.VMEM((3, 4, 2, 4, 32, 256), BF),
            pltpu.VMEM((3, 2, 4, 32, 256), BF),
            pltpu.VMEM((3, 2, 4, 32, 256), BF),
            pltpu.VMEM((16, 2048), F32),
            pltpu.VMEM((16, 2048), F32),
            pltpu.SemaphoreType.DMA((MOE_SEMS,)),
            pltpu.SemaphoreType.DMA((MOE_SEMS,)),
            pltpu.SemaphoreType.DMA((16,)),
        ],
        compiler_params=pltpu.CompilerParams(
            collective_id=1, has_side_effects=True, vmem_limit_bytes=60 * 2**20
        ),
        name="moe",
    )(*operands)


ATT_SEMS = 64


def attn_kernel(
    queries,
    keys,
    values,
    prefix_keys,
    prefix_values,
    out_weight,
    residual,
    gain,
    ids_in,
    gates_in,
    hidden,
    normed,
    meta_a,
    meta_b,
    q_raw,
    k_raw,
    v_raw,
    res_raw,
    gain_raw,
    ids,
    gates,
    res,
    kv,
    wts,
    qs,
    pre_k,
    pre_v,
    scores,
    pre_scores,
    top,
    summed,
    weighted,
    att,
    att_bf,
    own_term,
    core_send,
    core_recv,
    y_send,
    y_recv,
    x_keep,
    x_send,
    x_recv,
    info_a,
    info_b,
    send_sems,
    recv_sems,
    local_sems,
):
    x, y, z, core = place()
    other = 1 - core
    x_lo = x % 2
    kv_head = (lax.axis_index("expert")) // 4

    def at(dx=0, dy=0, dz=0, dc=0):
        return device((x + dx) % 4, (y + dy) % 4, (z + dz) % 8, (core + dc) % 2)

    sibling = at(dc=1)
    partner = device(x + 1 - 2 * x_lo, y, z, core)
    z_up, z_down = at(dz=1), at(dz=7)
    peers = [sibling, z_up, z_down, at(dz=2), at(dz=6)]
    for d in (1, 2, 3):
        peers.append(at(dx=d))
        peers.append(at(dy=d))
    arrived = greet(peers)
    head_cols = pl.ds(pl.multiple_of(kv_head * 128, 128), 128)
    loads = [
        pltpu.make_async_copy(src, dst, local_sems.at[i])
        for i, (src, dst) in enumerate(
            (
                (keys.at[:, :, head_cols], k_raw),
                (values.at[:, :, head_cols], v_raw),
                (ids_in, ids),
                (gates_in, gates),
                (out_weight, wts.at[0]),
                (queries, q_raw),
                (prefix_keys.at[:, head_cols], pre_k.at[0:64]),
                (prefix_values.at[:, head_cols], pre_v.at[0:64]),
                (residual, res_raw),
                (gain, gain_raw),
            )
        )
    ]
    for load in loads:
        load.start()
    for load in loads[:4]:
        load.wait()
    for b in range(2):
        kv[core, 0, :, b * 128 : (b + 1) * 128] = jnp.where(
            core == 0, k_raw[:, b, :].astype(F32), v_raw[:, b, :].astype(F32)
        ).astype(BF)
    token_ids = jnp.concatenate([ids[:, 0, :], ids[:, 1, :]], axis=0)
    token_gates = jnp.concatenate([gates[:, 0, :], gates[:, 1, :]], axis=0)
    lane = lax.broadcasted_iota(jnp.int32, (16, 128), 1)
    chosen = jnp.zeros((16, 128), F32)
    weight = jnp.zeros((16, 128), F32)
    for j in range(TOPK):
        column = token_ids[:, j : j + 1]
        chosen = chosen + jnp.where(lane == column, 1.0, 0.0)
        weight = weight + jnp.where(lane == column + 64, token_gates[:, j : j + 1], 0.0)
    row_i = lax.broadcasted_iota(jnp.int32, (16, 16), 0)
    col_i = lax.broadcasted_iota(jnp.int32, (16, 16), 1)
    lower = jnp.where(col_i <= row_i, 1.0, 0.0).astype(BF)
    rank = jnp.dot(lower, chosen.astype(BF), preferred_element_type=F32)
    own_rows = pl.ds(pl.multiple_of(core * 16, 16), 16)
    info_a[0, own_rows] = (rank * chosen + weight).astype(BF)

    links = Links(send_sems, recv_sems)
    arrived()

    def lines(dz):
        return pl.ds(dz * 32, 32)

    info = links.send(info_a.at[0, own_rows], info_a.at[0, own_rows], sibling)
    info_up, info_down = {}, {}

    def info_step(i):
        if i:
            info_up[i].wait_recv()
            info_down[i].wait_recv()
        else:
            info.wait_recv()
        if i < 3:
            src = info_a.at[0, lines((8 - i) % 8)]
            info_up[i + 1] = links.send(src, info_a.at[0, lines(7 - i)], z_up)
            info_down[i + 1] = links.send(
                info_a.at[0, lines(i)], info_a.at[0, lines(i + 1)], z_down
            )
        elif i == 3:
            low, high = pl.ds(4 * 32, 16), pl.ds(4 * 32 + 16, 16)
            info_up[4] = links.send(info_a.at[0, pl.ds(5 * 32, 16)], info_a.at[0, low], z_up)
            info_down[4] = links.send(info_a.at[0, pl.ds(3 * 32 + 16, 16)], info_a.at[0, high], z_down)


    across = {}
    sharing = links.used
    shared = [
        links.send_group([], kv.at[core, pl.ds(i * 8, 8)], kv.at[core, pl.ds(i * 8, 8)], sibling)
        for i in (0, 1)
    ]

    def share(block):
        links.more(sharing + block // 8, kv.at[core, block], kv.at[core, block], sibling)

    def hand_on(dz):
        share(dz)
        across[dz] = links.send(kv.at[core, dz], kv.at[core, 8 + dz], partner)

    def hand_over(dz):
        across[dz].wait_recv()
        share(8 + dz)

    w_up, w_down = {}, {}

    def w_start(s):
        r = pl.ds(s * 256, 256)
        w_up[s] = links.send(wts.at[0, r], wts.at[7, r], z_up)
        w_down[s] = links.send(wts.at[0, r], wts.at[1, r], z_down)

    def w_step(s, i):
        r = pl.ds(s * 256, 256)
        w_up[s].wait_recv()
        w_down[s].wait_recv()
        if i < 3:
            w_up[s] = links.send(wts.at[8 - i, r], wts.at[7 - i, r], z_up)
            w_down[s] = links.send(wts.at[i, r], wts.at[i + 1, r], z_down)
        elif i == 3:
            first, second = pl.ds(s * 256, 128), pl.ds(s * 256 + 128, 128)
            w_up[s] = links.send(wts.at[5, first], wts.at[4, first], z_up)
            w_down[s] = links.send(wts.at[3, second], wts.at[4, second], z_down)

    low, high = pl.ds(0, 64), pl.ds(64, 64)
    ring = {}
    for d in (1, 7, 2, 6):
        ring[8 - d] = links.send(kv.at[core, 0], kv.at[core, 8 - d], at(dz=d))
    hand_on(0)
    info_step(0)

    for load in loads[4:]:
        load.wait()
    for b in range(2):
        for h in range(4):
            qs[b, h * 128 : (h + 1) * 128, :] = q_raw[:, b, h * 128 : (h + 1) * 128]
    pre_k[64:128] = jnp.zeros((64, 128), BF)
    pre_v[64:128] = jnp.zeros((64, 128), BF)

    for dz in (7, 1):
        ring[dz].wait_recv()
        hand_on(dz)
    w_start(0)
    w_start(1)
    for dz, part, peer, far in ((6, low, z_up, at(dz=2)), (2, high, z_down, at(dz=6))):
        ring[dz].wait_recv()
        ring[5 if dz == 6 else 3] = links.send(
            kv.at[core, dz], kv.at[core, 5 if dz == 6 else 3], peer
        )
        ring[4, dz] = links.send(kv.at[core, dz, part], kv.at[core, 4, part], far)
        hand_on(dz)
    hand_over(0)
    info_step(1)
    hand_over(7)
    hand_over(1)
    info_step(2)
    for dz in (5, 3):
        ring[dz].wait_recv()
        hand_on(dz)
    ring[4, 6].wait_recv()
    ring[4, 2].wait_recv()
    hand_on(4)
    w_step(0, 1)
    hand_over(6)
    hand_over(2)
    w_step(1, 1)
    info_step(3)
    hand_over(5)
    hand_over(3)
    hand_over(4)
    info_step(4)
    info_moves = [
        links.send_group(
            [(info_a.at[0], dst.at[4 - d], at(**{axis: d})) for d in (1, 2, 3)],
            dst.at[1:4],
            dst.at[1:4],
        )
        for dst, axis in ((info_a, "dx"), (info_b, "dy"))
    ]
    for b in range(2):
        res[b * 8 : (b + 1) * 8] = res_raw[:, b, :].astype(F32)

    scale = 1.0 / math.sqrt(HD)
    gap = lax.broadcasted_iota(jnp.int32, (4, 128, 128), 2) - lax.broadcasted_iota(
        jnp.int32, (4, 128, 128), 1
    )
    gap = gap.reshape(512, 128)
    pre_lane = lax.broadcasted_iota(jnp.int32, (512, 128), 1)

    def attend_start(b):
        first = lax.dot_general(qs[b], pre_k[...], NT, preferred_element_type=F32) * scale
        first = jnp.where(pre_lane < 64, first, -1e30)
        pre_scores[b] = first
        top[b] = first

    def attend_scores(b, half):
        cols = slice(b * 128, (b + 1) * 128)

        def score(c, carry):
            block = lax.dot_general(
                qs[b],
                kv[0, pl.ds(2 * c, 2), :, cols].reshape(256, 128),
                NT,
                preferred_element_type=F32,
            )
            best = top[b]
            for r in range(2):
                theirs = ((x_lo + c // 4) % 2) * 8 + (z + 2 * c + r) % 8
                ahead = (x_lo * 8 + z - theirs) * 128
                part = jnp.where(gap <= ahead, block[:, r * 128 : (r + 1) * 128] * scale, -1e30)
                scores[b, c, :, r * 128 : (r + 1) * 128] = part
                best = jnp.maximum(best, part)
            top[b] = best
            return carry

        lax.fori_loop(half * 4, half * 4 + 4, score, 0)

    def attend_mix(b):
        cols = slice(b * 128, (b + 1) * 128)
        top[b] = jnp.broadcast_to(jnp.max(top[b], -1, keepdims=True), (512, 128))
        probs = jnp.exp(pre_scores[b] - top[b]).astype(BF)
        summed[...] = probs.astype(F32)
        weighted[...] = jnp.dot(probs, pre_v[...], preferred_element_type=F32)

        def mix(c, carry):
            peak = top[b]
            left = jnp.exp(scores[b, c, :, 0:128] - peak).astype(BF)
            right = jnp.exp(scores[b, c, :, 128:256] - peak).astype(BF)
            summed[...] += left.astype(F32) + right.astype(F32)
            weighted[...] += jnp.dot(
                jnp.concatenate([left, right], axis=1),
                kv[1, pl.ds(2 * c, 2), :, cols].reshape(256, 128),
                preferred_element_type=F32,
            )
            return carry

        lax.fori_loop(0, 8, mix, 0)
        result = weighted[...] / jnp.sum(summed[...], -1, keepdims=True)
        for h in range(4):
            for e in range(16):
                start = h * 128 + e * 8
                att[b, e % 2, (e // 2) % 4, e // 8, :, h * 128 : (h + 1) * 128] = result[
                    start : start + 8
                ]

        att_bf[0, b] = att[b].reshape(128, 512).astype(BF)
        return links.send(att_bf.at[0, b], att_bf.at[1, b], partner)

    attend_start(0)
    attend_start(1)
    shared[0].wait_recv()
    attend_scores(0, 0)
    attend_scores(1, 0)
    w_step(0, 2)
    w_step(1, 2)
    shared[1].wait_recv()
    attend_scores(0, 1)
    attend_scores(1, 1)
    w_step(0, 3)
    swaps = [attend_mix(0)]
    w_step(1, 3)
    swaps.append(attend_mix(1))
    for copy in info_moves:
        copy.wait_recv()
    meta_a[...] = info_a[...]
    meta_b[0] = info_a[0]
    meta_b[1:4] = info_b[1:4]
    for swap in swaps:
        swap.wait_recv()

    def half(c):
        rows = pl.ds(pl.multiple_of(c * 64, 64), 64)
        return att_bf[:, :, rows, :].reshape(256, 512)

    chunks = ((0, 7), (1, 6), (2, 5), (3, 4))
    core_moves, y_moves, x_moves = {}, {}, {}

    def project(j):
        if j == 3:
            w_step(0, 4)
            w_step(1, 4)
        for i, dz in enumerate(chunks[j]):
            cols = slice(i * 256, (i + 1) * 256)
            core_send[j, :, :, :, :, cols] = (
                jnp.dot(half(other), wts[dz], preferred_element_type=F32)
                .astype(BF)
                .reshape(2, 2, 4, 16, 256)
            )
        core_moves[j] = links.send(core_send.at[j], core_recv.at[j], sibling)
        for i, dz in enumerate(chunks[j]):
            cols = slice(i * 256, (i + 1) * 256)
            own_term[j, :, :, :, :, cols] = jnp.dot(
                half(core), wts[dz], preferred_element_type=F32
            ).reshape(2, 2, 4, 16, 256)

    def along_y(j):
        core_moves[j].wait_recv()
        both = own_term[j] + core_recv[j].astype(F32)
        own_term[j] = both
        y_send[j] = both.astype(BF)
        y_moves[j] = links.send_group(
            [
                (y_send.at[j, :, :, (y + d) % 4], y_recv.at[j, 4 - d], at(dy=d))
                for d in (2, 1, 3)
            ],
            y_recv.at[j, 1:4],
            y_recv.at[j, 1:4],
        )

    def along_x(j):
        own = own_term[j, :, :, y]
        y_moves[j].wait_recv()
        for d in (1, 2, 3):
            own = own + y_recv[j, d].astype(F32)
        for p in range(2):
            for i in range(2):
                tile = jnp.concatenate(
                    [own[p, 0, i * 8 : i * 8 + 8], own[p, 1, i * 8 : i * 8 + 8]], axis=0
                )
                x_keep[j, p, i] = tile
                x_send[j, p, i] = tile.astype(BF)
        x_moves[j] = links.send_group(
            [
                (x_send.at[j, d % 2, ((x + d) % 4) // 2], x_recv.at[j, 4 - d], at(dx=d))
                for d in (2, 1, 3)
            ],
            x_recv.at[j, 1:4],
            x_recv.at[j, 1:4],
        )

    square = jnp.zeros((16, 128), F32)

    def join(j, square):
        x_moves[j].wait_recv()
        mine = x_keep[j, 0, x // 2] + x_recv[j, 2].astype(F32)
        theirs = x_recv[j, 1].astype(F32) + x_recv[j, 3].astype(F32)
        for i, dz in enumerate(chunks[j]):
            for side, part in ((x_lo, mine), (1 - x_lo, theirs)):
                where = pl.ds(pl.multiple_of((side * 8 + (z + dz) % 8) * 256, 256), 256)
                value = res[:, where] + part[:, i * 256 : (i + 1) * 256]
                hidden[:, where] = value
                value = value * value
                square = square + value[:, 0:128] + value[:, 128:256]
        return square

    project(0)
    project(1)
    along_y(0)
    project(2)
    along_y(1)
    project(3)
    along_y(2)
    along_x(0)
    along_y(3)
    for j in (1, 2, 3):
        along_x(j)
    for j in range(4):
        square = join(j, square)
    mean = jnp.sum(square, -1, keepdims=True) * (1.0 / D)
    normed[...] = (hidden[...] * lax.rsqrt(mean + 1e-06) * gain_raw[...].reshape(1, D).astype(F32)).astype(BF)
    links.finish()


def attention(*operands):
    vmem = pl.BlockSpec(memory_space=pltpu.VMEM)
    hbm = pl.BlockSpec(memory_space=pl.ANY)
    return pl.pallas_call(
        attn_kernel,
        out_shape=(
            jax.ShapeDtypeStruct((16, D), F32),
            jax.ShapeDtypeStruct((16, D), BF),
            jax.ShapeDtypeStruct((4, 256, 128), BF),
            jax.ShapeDtypeStruct((4, 256, 128), BF),
        ),
        in_specs=[hbm] * 10,
        out_specs=(vmem,) * 4,
        scratch_shapes=[
            pltpu.VMEM((128, 2, 512), BF),
            pltpu.VMEM((128, 2, 128), BF),
            pltpu.VMEM((128, 2, 128), BF),
            pltpu.VMEM((8, 2, D), BF),
            pltpu.VMEM((D,), BF),
            pltpu.VMEM((8, 2, TOPK), jnp.int32),
            pltpu.VMEM((8, 2, TOPK), F32),
            pltpu.VMEM((16, D), F32),
            pltpu.VMEM((2, 16, 128, 256), BF),
            pltpu.VMEM((8, 512, 256), BF),
            pltpu.VMEM((2, 512, 128), BF),
            pltpu.VMEM((128, 128), BF),
            pltpu.VMEM((128, 128), BF),
            pltpu.VMEM((2, 8, 512, 256), F32),
            pltpu.VMEM((2, 512, 128), F32),
            pltpu.VMEM((2, 512, 128), F32),
            pltpu.VMEM((512, 128), F32),
            pltpu.VMEM((512, 128), F32),
            pltpu.VMEM((2, 2, 4, 2, 8, 512), F32),
            pltpu.VMEM((2, 2, 128, 512), BF),
            pltpu.VMEM((4, 2, 2, 4, 16, 512), F32),
            pltpu.VMEM((4, 2, 2, 4, 16, 512), BF),
            pltpu.VMEM((4, 2, 2, 4, 16, 512), BF),
            pltpu.VMEM((4, 2, 2, 4, 16, 512), BF),
            pltpu.VMEM((4, 4, 2, 2, 16, 512), BF),
            pltpu.VMEM((4, 2, 2, 16, 512), F32),
            pltpu.VMEM((4, 2, 2, 16, 512), BF),
            pltpu.VMEM((4, 4, 16, 512), BF),
            pltpu.VMEM((4, 256, 128), BF),
            pltpu.VMEM((4, 256, 128), BF),
            pltpu.SemaphoreType.DMA((ATT_SEMS,)),
            pltpu.SemaphoreType.DMA((ATT_SEMS,)),
            pltpu.SemaphoreType.DMA((10,)),
        ],
        compiler_params=pltpu.CompilerParams(
            collective_id=2, has_side_effects=True, vmem_limit_bytes=60 * 2**20
        ),
        name="attention",
    )(*operands)


def shards(
    queries,
    keys,
    values,
    prefix_keys,
    prefix_values,
    out_weight,
    residual_in,
    norm_gain,
    expert_ids,
    route_weights,
    w_gate,
    w_up,
    w_down,
):
    hidden_state, normed, meta_a, meta_b = attention(
        queries,
        keys,
        values,
        prefix_keys,
        prefix_values,
        out_weight,
        residual_in,
        norm_gain,
        expert_ids,
        route_weights,
    )
    return moe(
        normed, meta_a, meta_b, hidden_state, w_gate[0, 0], w_up[0, 0], w_down[0, 0]
    )


def solution(mesh):
    in_specs = (
        P("seq", None, "expert"),
        P("seq", None, None),
        P("seq", None, None),
        P(),
        P(),
        P("expert", "seq"),
        P(("seq", "expert"), None, None),
        P(),
        P(("seq", "expert"), None, None),
        P(("seq", "expert"), None, None),
        P("seq", "expert", None, None),
        P("seq", "expert", None, None),
        P("seq", "expert", None, None),
    )
    out_specs = P(("seq", "expert"), None, None)
    return jax.shard_map(shards, mesh=mesh, in_specs=in_specs, out_specs=out_specs, check_vma=False)
```

```python
import math

import jax
import jax.numpy as jnp
from jax import lax
from jax.experimental import pallas as pl
from jax.experimental.pallas import tpu as pltpu
from jax.sharding import PartitionSpec as P

D = 4096
HD = 128
TOPK = 8

MESH = pl.DeviceIdType.MESH
BF = jnp.bfloat16
F32 = jnp.float32
NT = (((1,), (1,)), ((), ()))
ORDER = (0, 1, 3, 2)
SPOS = {0: 0, 1: 1, 3: 2, 2: 3}
MOE_SEMS = 104
FAR = (1, 2, 3)


def place():
    s = lax.axis_index("seq")
    e = lax.axis_index("expert")
    return (e // 8) * 2 + s // 8, (e // 2) % 4, s % 8, e % 2


def device(x, y, z, c):
    return ((x % 2) * 8 + z, ((x // 2) * 4 + y) * 2 + c)


class Links:
    def __init__(self, send_sems, recv_sems):
        self.send_sems = send_sems
        self.recv_sems = recv_sems
        self.used = 0
        self.open = []

    def copy(self, src, dst, peer, index):
        return pltpu.make_async_remote_copy(
            src_ref=src,
            dst_ref=dst,
            send_sem=self.send_sems.at[index],
            recv_sem=self.recv_sems.at[index],
            device_id=peer,
            device_id_type=MESH,
        )

    def send(self, src, dst, peer):
        copy = self.copy(src, dst, peer, self.used)
        self.used += 1
        copy.start()
        self.open.append(copy)
        return copy

    def send_group(self, copies, all_src, all_dst, peer=None):
        index = self.used
        self.used += 1
        for src, dst, to in copies:
            self.copy(src, dst, to, index).start()
        group = self.copy(all_src, all_dst, peer or copies[0][2], index)
        self.open.append(group)
        return group

    def more(self, index, src, dst, peer):
        self.copy(src, dst, peer, index).start()

    def finish(self):
        for copy in self.open:
            copy.wait_send()
        self.open = []


def greet(peers):
    barrier = pltpu.get_barrier_semaphore()
    for peer in peers:
        pl.semaphore_signal(barrier, inc=1, device_id=peer, device_id_type=MESH)
    return lambda: pl.semaphore_wait(barrier, len(peers))


def moe_kernel(
    normed,
    meta_a,
    meta_b,
    hidden,
    w_gate,
    w_up,
    w_down,
    out,
    mix,
    tok,
    stage,
    near,
    far,
    far_stage,
    slot,
    got,
    back,
    acc,
    hid,
    w_in,
    w_out,
    rank_mask,
    rank_mask_t,
    choose,
    scatter,
    part_send,
    part_recv,
    total,
    z_send,
    z_recv,
    far_total,
    far_send,
    far_plus,
    far_minus,
    line_send,
    line_recv,
    core_send,
    core_recv,
    send_sems,
    recv_sems,
    local_sems,
):
    x, y, z, core = place()
    other = 1 - core

    def at(dx=0, dy=0, dz=0, dc=0):
        return device((x + dx) % 4, (y + dy) % 4, (z + dz) % 8, (core + dc) % 2)

    def line(h, d):
        return at(dy=d) if h else at(dx=d)

    def toward(h, d, dc):
        return at(dx=d, dc=dc) if h else at(dy=d, dc=dc)

    sibling = at(dc=1)
    z_up, z_down = at(dz=1), at(dz=7)
    peers = [sibling] + [at(dz=d, dc=dc) for d in range(1, 8) for dc in (0, 1)]
    for d in (1, 2, 3):
        for dc in (0, 1):
            peers.append(at(dx=d, dc=dc))
            peers.append(at(dy=d, dc=dc))
    arrived = greet(peers)
    loads = [
        pltpu.make_async_copy(w_gate, w_in.at[:, 0:384], local_sems.at[0]),
        pltpu.make_async_copy(w_up, w_in.at[:, 384:768], local_sems.at[1]),
        pltpu.make_async_copy(w_down, w_out, local_sems.at[2]),
    ]
    for load in loads:
        load.start()

    def columns(k, h, c):
        return pl.ds(pl.multiple_of(k * 2048 + h * 1024 + c * 256, 256), 256)

    own_rows = pl.ds(pl.multiple_of(core * 16, 16), 16)
    for h in (0, 1):
        cols = slice(h * 256, (h + 1) * 256)
        stage[:, cols] = normed[:, columns(other, h, 0)]
        tok[own_rows, cols] = normed[:, columns(core, h, 0)]
        for c in FAR:
            far_stage[c - 1, h] = normed[:, columns(other, h, c)]
            far[c - 1, h, 0, 0, own_rows] = normed[:, columns(core, h, c)]

    links = Links(send_sems, recv_sems)
    arrived()
    def own_at(dz):
        return pl.ds(pl.multiple_of(dz * 32 + core * 16, 16), 16)

    swap = links.send(stage, tok.at[own_rows], sibling)
    ring = {}
    for d in (1, 7, 2, 6, 3, 5, 4):
        whole = tok.at[pl.ds((8 - d) * 32, 32)]
        ring[8 - d] = links.send_group(
            [
                (src, tok.at[own_at(8 - d)], at(dz=d, dc=dc))
                for dc, src in ((0, tok.at[own_rows]), (1, stage))
            ],
            whole,
            whole,
        )
    far_swap = links.send(far_stage, far.at[:, :, 0, 0, own_rows], sibling)
    swap.wait_recv()

    def rows(dz):
        return pl.ds(dz * 32, 32)

    dense = {}

    def spread(dz):
        r = rows(dz)
        dense[dz] = links.send_group(
            [
                (tok.at[r, h * 256 : (h + 1) * 256], near.at[h, 4 - d, r], line(h, d))
                for d in (2, 1, 3)
                for h in (0, 1)
            ],
            near.at[:, 1:4, r],
            near.at[:, 1:4, r],
        )

    spread(0)
    far_swap.wait_recv()
    far_line = links.send_group(
        [
            (far.at[:, h, 0, 0], far.at[:, h, 0, 4 - d], line(h, d))
            for d in (2, 1, 3)
            for h in (0, 1)
        ],
        far.at[:, :, 0, 1:4],
        far.at[:, :, 0, 1:4],
    )

    n = lax.broadcasted_iota(jnp.int32, (8, 48, 256), 1)
    t = lax.broadcasted_iota(jnp.int32, (8, 48, 256), 2)
    block = (n * 171) >> 9
    rank_mask[...] = (
        jnp.where(block == (t >> 4), n - 3 * block + 1, -1).astype(F32).reshape(384, 256)
    )
    r = lax.broadcasted_iota(jnp.int32, (256, 384), 1)
    t = lax.broadcasted_iota(jnp.int32, (256, 384), 0)
    n = r - 48 * ((r * 1366) >> 16)
    block = (n * 171) >> 9
    rank_mask_t[...] = jnp.where(block == (t >> 4), n - 3 * block + 1, -1).astype(F32)
    q = lax.broadcasted_iota(jnp.int32, (8, 48, 128), 0)
    lane = lax.broadcasted_iota(jnp.int32, (8, 48, 128), 2)
    step = q >> 1
    to_core = (core + (q & 1)) & 1
    to_y = (y + step) & 3
    to_x = (x + step) & 3
    half = z // 4
    expert_a = 4 * ((x // 2 * 4 + to_y) * 2 + to_core) + 2 * (x % 2) + half
    expert_b = 4 * (((to_x >> 1) * 4 + y) * 2 + to_core) + 2 * (to_x & 1) + half
    metas = (meta_a, meta_b)

    def one_hot(match):
        return jnp.where(match, 1.0, 0.0).astype(BF).reshape(384, 128)

    def masks(h, d):
        expert = expert_b if h else expert_a
        pick = one_hot(lane == expert)
        info = metas[h][d]
        found = lax.dot_general(pick, info, NT, preferred_element_type=F32)
        choose[h, d] = jnp.where(found == rank_mask[...], 1.0, 0.0).astype(BF)
        found = lax.dot_general(info, pick, NT, preferred_element_type=F32)
        scale = lax.dot_general(info, one_hot(lane == expert + 64), NT, preferred_element_type=F32)
        scatter[h, d] = jnp.where(found == rank_mask_t[...], scale, 0.0).astype(BF)

    far_up, far_down = {}, {}

    def far_start(c):
        piece = far.at[c - 1]
        far_up[c] = links.send(piece.at[:, 0], piece.at[:, 7], z_up)
        far_down[c] = links.send(piece.at[:, 0], piece.at[:, 1], z_down)

    def far_step(c, i):
        piece = far.at[c - 1]
        far_up[c].wait_recv()
        far_down[c].wait_recv()
        if i < 3:
            far_up[c] = links.send(piece.at[:, 8 - i], piece.at[:, 7 - i], z_up)
            far_down[c] = links.send(piece.at[:, i], piece.at[:, i + 1], z_down)
        elif i == 3:
            left, right = pl.ds(0, 2), pl.ds(2, 2)
            far_up[c] = links.send(piece.at[:, 5, left], piece.at[:, 4, left], z_up)
            far_down[c] = links.send(piece.at[:, 3, right], piece.at[:, 4, right], z_down)

    masks(0, 0)
    masks(1, 0)
    for dz in (7, 1):
        ring[dz].wait_recv()
        spread(dz)
    far_line.wait_recv()
    far_start(1)
    for dz in (6, 2, 5, 3, 4):
        ring[dz].wait_recv()
        spread(dz)
    far_start(2)
    masks(0, 1)
    masks(1, 1)
    masks(0, 3)
    far_step(1, 1)
    masks(1, 3)
    masks(0, 2)
    masks(1, 2)
    acc[...] = jnp.zeros_like(acc)

    def select(c, h, d):
        if c:
            tokens = far[c - 1, h, :, d].reshape(256, 256)
        elif d == 0:
            tokens = tok[:, h * 256 : (h + 1) * 256]
        else:
            tokens = near[h, d]
        picked = jnp.dot(choose[h, d], tokens, preferred_element_type=F32)
        slot[c, h, SPOS[d]] = picked.astype(BF).reshape(8, 48, 256)

    moved, kept = {}, {}

    def dispatch(c, h):
        for d in (0, 1, 3, 2):
            select(c, h, d)
        copies = []
        for d in (2, 1, 3, 0):
            for dc in (0, 1):
                src = slot.at[c, h, :, d * 2 + dc]
                dst = got.at[c, h, ((4 - d) % 4) * 2 + dc]
                if d == 0 and dc == 0:
                    kept[c, h] = pltpu.make_async_copy(src, dst, local_sems.at[3 + c * 2 + h])
                    kept[c, h].start()
                else:
                    copies.append((src, dst, toward(h, d, dc)))
        moved[c, h] = links.send_group(copies, slot.at[c, h, :, 1:8], got.at[c, h, 1:8])

    def expert_in(c, h):
        kept[c, h].wait()
        moved[c, h].wait_recv()
        for d in (0, 1, 3, 2):
            term = 0
            for dc in (0, 1):
                k = (core + dc) % 2
                term = term + jnp.dot(
                    got[c, h, d * 2 + dc].reshape(192, 256),
                    w_in[columns(k, h, c), :],
                    preferred_element_type=F32,
                )
            if h == 0:
                acc[:, SPOS[d]] += term.reshape(4, 48, 768)
            else:
                acc[SPOS[d]] += term.reshape(4, 48, 768)

    for dz in range(8):
        dense[dz].wait_recv()
    dispatch(0, 0)
    far_step(1, 2)
    dispatch(0, 1)
    far_step(2, 1)
    far_step(1, 3)
    far_start(3)
    for load in loads:
        load.wait()
    far_step(2, 2)
    far_step(1, 4)
    dispatch(1, 0)
    far_step(2, 3)
    far_step(3, 1)
    dispatch(1, 1)
    expert_in(0, 0)
    far_step(2, 4)
    far_step(3, 2)
    dispatch(2, 0)
    dispatch(2, 1)
    far_step(3, 3)
    expert_in(0, 1)
    far_step(3, 4)
    dispatch(3, 0)
    dispatch(3, 1)
    for c in FAR:
        for h in (0, 1):
            expert_in(c, h)
    for i in range(4):
        gate = acc[i, :, :, 0:384]
        hid[i] = (gate / (1.0 + jnp.exp(-gate)) * acc[i, :, :, 384:768]).astype(BF)

    returned = {}

    def expert_out(c, h):
        index = links.used
        returned[c, h] = links.send_group(
            [], got.at[c, h, 1:8], back.at[c, h, :, 1:8], sibling
        )
        for d in (2, 1, 3, 0):
            rows_in = hid[:, SPOS[d]] if h == 0 else hid[SPOS[d]]
            for dc in (0, 1):
                k = (core + dc) % 2
                block_out = (
                    jnp.dot(
                        rows_in.reshape(192, 384),
                        w_out[:, columns(k, h, c)],
                        preferred_element_type=F32,
                    )
                    .astype(BF)
                    .reshape(4, 48, 256)
                )
                if d == 0 and dc == 0:
                    back[c, h, :, 0] = block_out
                    continue
                target = ((4 - d) % 4) * 2 + dc
                got[c, h, d * 2 + dc] = block_out
                links.more(
                    index, got.at[c, h, d * 2 + dc], back.at[c, h, :, target], toward(h, d, dc)
                )

    def combine(c, h, d):
        return jnp.dot(
            scatter[h, d], back[c, h, SPOS[d]].reshape(384, 256), preferred_element_type=F32
        )

    def all_back(c, h):
        returned[c, h].wait_recv()

    def far_open(c):
        for h in (0, 1):
            all_back(c, h)
            for d in range(4):
                far_total[c - 1, h, d] = combine(c, h, d)
        send, left, right = far_send.at[c - 1], pl.ds(0, 2), pl.ds(2, 2)
        send[:, 4] = far_total[c - 1, :, :, 128:160].astype(BF)
        far_up[c] = links.send(send.at[:, 4, left], far_plus.at[c - 1, 3, :, left], z_up)
        far_down[c] = links.send(send.at[:, 4, right], far_minus.at[c - 1, 3, :, right], z_down)

    def far_return(c, i):
        rest = 8 - i
        left, right = slice(0, 2), slice(2, 4)
        send, plus, minus = far_send.at[c - 1], far_plus.at[c - 1], far_minus.at[c - 1]

        def mine(dz, span=slice(0, 4)):
            return far_total[c - 1, :, span, dz * 32 : dz * 32 + 32]

        far_up[c].wait_recv()
        if i == 3:
            send[:, i, left] = (mine(i, left) + plus[i, :, left].astype(F32)).astype(BF)
            send[:, i, right] = mine(i, right).astype(BF)
        else:
            send[:, i] = (mine(i) + plus[i].astype(F32)).astype(BF)
        far_up[c] = links.send(send.at[:, i], plus.at[i - 1], z_up)
        far_down[c].wait_recv()
        if i == 3:
            send[:, rest, left] = mine(rest, left).astype(BF)
            send[:, rest, right] = (mine(rest, right) + minus[i, :, right].astype(F32)).astype(BF)
        else:
            send[:, rest] = (mine(rest) + minus[i].astype(F32)).astype(BF)
        far_down[c] = links.send(send.at[:, rest], minus.at[i - 1], z_down)

    line_moves = {}

    def far_finish(c):
        far_up[c].wait_recv()
        far_down[c].wait_recv()
        ends = (
            far_total[c - 1, :, :, 0:32]
            + far_plus[c - 1, 0].astype(F32)
            + far_minus[c - 1, 0].astype(F32)
        )
        line_send[c - 1] = ends.astype(BF)
        line_moves[c] = links.send_group(
            [
                (line_send.at[c - 1, h, d], line_recv.at[c - 1, h, (4 - d) % 4], line(h, d))
                for d in (2, 1, 3)
                for h in (0, 1)
            ],
            line_send.at[c - 1, :, 1:4],
            line_recv.at[c - 1, :, 1:4],
        )
        far_total[c - 1, :, 0, 0:32] = ends[:, 0]

    def far_join(c):
        line_moves[c].wait_recv()
        for d in (1, 2, 3):
            far_total[c - 1, :, 0, 0:32] += line_recv[c - 1, :, d].astype(F32)

    parts = {}

    def near_part(h):
        all_back(0, h)
        index = links.used
        parts[h] = links.send_group([], part_send.at[h, 1:4], part_recv.at[h, 1:4], line(h, 1))
        for d in (2, 1, 3):
            part_send[h, d] = combine(0, h, d).astype(BF)
            links.more(index, part_send.at[h, d], part_recv.at[h, 4 - d], line(h, d))
        total[:, h * 256 : (h + 1) * 256] = combine(0, h, 0)

    def near_join(h):
        parts[h].wait_recv()
        rest = part_recv[h, 1].astype(F32) + part_recv[h, 2].astype(F32)
        total[:, h * 256 : (h + 1) * 256] += rest + part_recv[h, 3].astype(F32)

    def z_return():
        z_send[...] = total[...].reshape(8, 2, 16, 512).astype(BF)
        far_side = links.send_group(
            [
                (z_send.at[d, (core + dc) % 2], z_recv.at[8 - d, dc], at(dz=d, dc=dc))
                for d in (4, 3, 5, 2, 6, 1, 7)
                for dc in (0, 1)
            ],
            z_send.at[1:8],
            z_recv.at[1:8],
        )
        return far_side, links.send(z_send.at[0, other], z_recv.at[0, 1], sibling)

    for c in (1, 2):
        for h in (0, 1):
            expert_out(c, h)
    far_open(1)
    expert_out(3, 0)
    far_return(1, 3)
    expert_out(3, 1)
    far_return(1, 2)
    far_open(2)
    far_return(1, 1)
    expert_out(0, 0)
    far_return(2, 3)
    expert_out(0, 1)
    far_finish(1)
    far_return(2, 2)
    far_open(3)
    far_return(2, 1)
    far_return(3, 3)
    near_part(0)
    near_part(1)
    far_return(3, 2)
    far_finish(2)
    far_return(3, 1)
    near_join(0)
    near_join(1)
    ending = z_return()
    far_join(1)
    far_join(2)
    far_finish(3)
    far_join(3)
    other_rows = pl.ds(pl.multiple_of(other * 16, 16), 16)
    for h in (0, 1):
        for c in FAR:
            core_send[h * 3 + c - 1] = far_total[c - 1, h, 0, other_rows].astype(BF)
    swap = links.send(core_send, core_recv, sibling)
    for h in (0, 1):
        for c in FAR:
            mix[:, columns(core, h, c)] = far_total[c - 1, h, 0, own_rows]
    swap.wait_recv()
    for h in (0, 1):
        for c in FAR:
            mix[:, columns(other, h, c)] = core_recv[h * 3 + c - 1].astype(F32)
    for copy in ending:
        copy.wait_recv()
    ends = total[own_rows]
    beside = z_recv[0, 1].astype(F32)
    for d in range(1, 8):
        ends = ends + z_recv[d, 0].astype(F32)
        beside = beside + z_recv[d, 1].astype(F32)
    for h in (0, 1):
        mix[:, columns(core, h, 0)] = ends[:, h * 256 : (h + 1) * 256]
        mix[:, columns(other, h, 0)] = beside[:, h * 256 : (h + 1) * 256]
    result = hidden[...] + mix[...]
    out[...] = jnp.stack([result[0:8], result[8:16]], axis=1).astype(BF)
    assert links.used <= MOE_SEMS
    links.finish()


def moe(*operands):
    vmem = pl.BlockSpec(memory_space=pltpu.VMEM)
    hbm = pl.BlockSpec(memory_space=pl.ANY)
    return pl.pallas_call(
        moe_kernel,
        out_shape=jax.ShapeDtypeStruct((8, 2, D), BF),
        in_specs=[vmem, vmem, vmem, vmem, hbm, hbm, hbm],
        out_specs=vmem,
        scratch_shapes=[
            pltpu.VMEM((16, D), F32),
            pltpu.VMEM((256, 512), BF),
            pltpu.VMEM((16, 512), BF),
            pltpu.VMEM((2, 4, 256, 256), BF),
            pltpu.VMEM((3, 2, 8, 4, 32, 256), BF),
            pltpu.VMEM((3, 2, 16, 256), BF),
            pltpu.VMEM((4, 2, 4, 8, 48, 256), BF),
            pltpu.VMEM((4, 2, 8, 4, 48, 256), BF),
            pltpu.VMEM((4, 2, 4, 8, 48, 256), BF),
            pltpu.VMEM((4, 4, 48, 768), F32),
            pltpu.VMEM((4, 4, 48, 384), BF),
            pltpu.VMEM((4096, 768), BF),
            pltpu.VMEM((384, 4096), BF),
            pltpu.VMEM((384, 256), F32),
            pltpu.VMEM((256, 384), F32),
            pltpu.VMEM((2, 4, 384, 256), BF),
            pltpu.VMEM((2, 4, 256, 384), BF),
            pltpu.VMEM((2, 4, 256, 256), BF),
            pltpu.VMEM((2, 4, 256, 256), BF),
            pltpu.VMEM((256, 512), F32),
            pltpu.VMEM((8, 2, 16, 512), BF),
            pltpu.VMEM((8, 2, 16, 512), BF),
            pltpu.VMEM((3, 2, 4, 256, 256), F32),
            pltpu.VMEM((3, 2, 8, 4, 32, 256), BF),
            pltpu.VMEM((3, 4, 2, 4, 32, 256), BF),
            pltpu.VMEM((3, 4, 2, 4, 32, 256), BF),
            pltpu.VMEM((3, 2, 4, 32, 256), BF),
            pltpu.VMEM((3, 2, 4, 32, 256), BF),
            pltpu.VMEM((6, 16, 256), BF),
            pltpu.VMEM((6, 16, 256), BF),
            pltpu.SemaphoreType.DMA((MOE_SEMS,)),
            pltpu.SemaphoreType.DMA((MOE_SEMS,)),
            pltpu.SemaphoreType.DMA((16,)),
        ],
        compiler_params=pltpu.CompilerParams(
            collective_id=1, has_side_effects=True, vmem_limit_bytes=60 * 2**20
        ),
        name="moe",
    )(*operands)


ATT_SEMS = 80


def attn_kernel(
    queries,
    keys,
    values,
    prefix_keys,
    prefix_values,
    out_weight,
    residual,
    gain,
    ids_in,
    gates_in,
    hidden,
    normed,
    meta_a,
    meta_b,
    q_raw,
    k_raw,
    v_raw,
    res_raw,
    gain_raw,
    ids,
    gates,
    res,
    kv,
    wts,
    qs,
    pre_k,
    pre_v,
    scores,
    pre_scores,
    top,
    summed,
    weighted,
    att,
    att_bf,
    own_term,
    core_send,
    core_recv,
    y_send,
    y_recv,
    x_keep,
    x_send,
    x_recv,
    info_a,
    info_b,
    send_sems,
    recv_sems,
    local_sems,
):
    x, y, z, core = place()
    other = 1 - core
    x_lo = x % 2
    kv_head = (lax.axis_index("expert")) // 4

    def at(dx=0, dy=0, dz=0, dc=0):
        return device((x + dx) % 4, (y + dy) % 4, (z + dz) % 8, (core + dc) % 2)

    sibling = at(dc=1)
    partner = device(x + 1 - 2 * x_lo, y, z, core)
    y_partner = device(x, y + 1 - 2 * (y % 2), z, core)
    mine = pl.ds(pl.multiple_of((y % 2) * 64, 64), 64)
    theirs = pl.ds(pl.multiple_of((1 - y % 2) * 64, 64), 64)
    z_up, z_down = at(dz=1), at(dz=7)
    peers = [sibling, z_up, z_down, at(dz=2), at(dz=6)]
    for d in (1, 2, 3):
        peers.append(at(dx=d))
        peers.append(at(dy=d))
    arrived = greet(peers)
    head_cols = pl.ds(pl.multiple_of(kv_head * 128, 128), 128)
    loads = [
        pltpu.make_async_copy(src, dst, local_sems.at[i])
        for i, (src, dst) in enumerate(
            (
                (keys.at[:, :, head_cols], k_raw),
                (values.at[:, :, head_cols], v_raw),
                (ids_in, ids),
                (gates_in, gates),
                (out_weight, wts.at[0]),
                (queries, q_raw),
                (prefix_keys.at[:, head_cols], pre_k.at[0:64]),
                (prefix_values.at[:, head_cols], pre_v.at[0:64]),
                (residual, res_raw),
                (gain, gain_raw),
            )
        )
    ]
    for load in loads:
        load.start()
    for load in loads[:4]:
        load.wait()
    for b in range(2):
        kv[core, 0, :, b * 128 : (b + 1) * 128] = jnp.where(
            core == 0, k_raw[:, b, :].astype(F32), v_raw[:, b, :].astype(F32)
        ).astype(BF)
    token_ids = jnp.concatenate([ids[:, 0, :], ids[:, 1, :]], axis=0)
    token_gates = jnp.concatenate([gates[:, 0, :], gates[:, 1, :]], axis=0)
    lane = lax.broadcasted_iota(jnp.int32, (16, 128), 1)
    chosen = jnp.zeros((16, 128), F32)
    weight = jnp.zeros((16, 128), F32)
    for j in range(TOPK):
        column = token_ids[:, j : j + 1]
        chosen = chosen + jnp.where(lane == column, 1.0, 0.0)
        weight = weight + jnp.where(lane == column + 64, token_gates[:, j : j + 1], 0.0)
    row_i = lax.broadcasted_iota(jnp.int32, (16, 16), 0)
    col_i = lax.broadcasted_iota(jnp.int32, (16, 16), 1)
    lower = jnp.where(col_i <= row_i, 1.0, 0.0).astype(BF)
    rank = jnp.dot(lower, chosen.astype(BF), preferred_element_type=F32)
    own_rows = pl.ds(pl.multiple_of(core * 16, 16), 16)
    info_a[0, own_rows] = (rank * chosen + weight).astype(BF)

    links = Links(send_sems, recv_sems)
    arrived()

    def lines(dz):
        return pl.ds(dz * 32, 32)

    info = links.send(info_a.at[0, own_rows], info_a.at[0, own_rows], sibling)
    info_up, info_down = {}, {}

    def info_step(i):
        if i:
            info_up[i].wait_recv()
            info_down[i].wait_recv()
        else:
            info.wait_recv()
        if i < 3:
            src = info_a.at[0, lines((8 - i) % 8)]
            info_up[i + 1] = links.send(src, info_a.at[0, lines(7 - i)], z_up)
            info_down[i + 1] = links.send(
                info_a.at[0, lines(i)], info_a.at[0, lines(i + 1)], z_down
            )
        elif i == 3:
            low, high = pl.ds(4 * 32, 16), pl.ds(4 * 32 + 16, 16)
            info_up[4] = links.send(info_a.at[0, pl.ds(5 * 32, 16)], info_a.at[0, low], z_up)
            info_down[4] = links.send(info_a.at[0, pl.ds(3 * 32 + 16, 16)], info_a.at[0, high], z_down)


    across, beside = {}, {}
    sharing = links.used
    shared = [
        links.send_group([], kv.at[core, pl.ds(i * 8, 8)], kv.at[core, pl.ds(i * 8, 8)], sibling)
        for i in (0, 1)
    ]

    def share(block, rows=pl.ds(0, 128)):
        piece = kv.at[core, block, rows]
        links.more(sharing + block // 8, piece, piece, sibling)

    def hand_on(dz):
        share(dz)
        across[dz] = links.send(kv.at[core, dz, mine], kv.at[core, 8 + dz, mine], partner)

    def hand_over(dz):
        across[dz].wait_recv()
        piece = kv.at[core, 8 + dz, mine]
        beside[dz] = links.send(piece, piece, y_partner)
        share(8 + dz, mine)

    def hand_last(dz):
        beside[dz].wait_recv()
        share(8 + dz, theirs)

    w_up, w_down = {}, {}

    def w_start(s):
        r = pl.ds(s * 256, 256)
        w_up[s] = links.send(wts.at[0, r], wts.at[7, r], z_up)
        w_down[s] = links.send(wts.at[0, r], wts.at[1, r], z_down)

    def w_step(s, i):
        r = pl.ds(s * 256, 256)
        w_up[s].wait_recv()
        w_down[s].wait_recv()
        if i < 3:
            w_up[s] = links.send(wts.at[8 - i, r], wts.at[7 - i, r], z_up)
            w_down[s] = links.send(wts.at[i, r], wts.at[i + 1, r], z_down)
        elif i == 3:
            first, second = pl.ds(s * 256, 128), pl.ds(s * 256 + 128, 128)
            w_up[s] = links.send(wts.at[5, first], wts.at[4, first], z_up)
            w_down[s] = links.send(wts.at[3, second], wts.at[4, second], z_down)

    low, high = pl.ds(0, 64), pl.ds(64, 64)
    ring = {}
    for d in (1, 7, 2, 6):
        ring[8 - d] = links.send(kv.at[core, 0], kv.at[core, 8 - d], at(dz=d))
    hand_on(0)
    info_step(0)

    for load in loads[4:]:
        load.wait()
    for b in range(2):
        for h in range(4):
            qs[b, h * 128 : (h + 1) * 128, :] = q_raw[:, b, h * 128 : (h + 1) * 128]
    pre_k[64:128] = jnp.zeros((64, 128), BF)
    pre_v[64:128] = jnp.zeros((64, 128), BF)

    for dz in (7, 1):
        ring[dz].wait_recv()
        hand_on(dz)
    w_start(0)
    w_start(1)
    for dz, part, peer, far in ((6, low, z_up, at(dz=2)), (2, high, z_down, at(dz=6))):
        ring[dz].wait_recv()
        ring[5 if dz == 6 else 3] = links.send(
            kv.at[core, dz], kv.at[core, 5 if dz == 6 else 3], peer
        )
        ring[4, dz] = links.send(kv.at[core, dz, part], kv.at[core, 4, part], far)
        hand_on(dz)
    hand_over(0)
    info_step(1)
    hand_over(7)
    hand_over(1)
    hand_last(0)
    info_step(2)
    for dz in (5, 3):
        ring[dz].wait_recv()
        hand_on(dz)
    ring[4, 6].wait_recv()
    ring[4, 2].wait_recv()
    hand_on(4)
    hand_over(6)
    hand_over(2)
    hand_last(7)
    hand_last(1)
    w_step(0, 1)
    info_step(3)
    hand_over(5)
    hand_over(3)
    hand_last(6)
    hand_last(2)
    w_step(1, 1)
    hand_over(4)
    info_step(4)
    hand_last(5)
    hand_last(3)
    info_moves = [
        links.send_group(
            [(info_a.at[0], dst.at[4 - d], at(**{axis: d})) for d in (1, 2, 3)],
            dst.at[1:4],
            dst.at[1:4],
        )
        for dst, axis in ((info_a, "dx"), (info_b, "dy"))
    ]
    for b in range(2):
        res[b * 8 : (b + 1) * 8] = res_raw[:, b, :].astype(F32)

    scale = 1.0 / math.sqrt(HD)
    gap = lax.broadcasted_iota(jnp.int32, (4, 128, 128), 2) - lax.broadcasted_iota(
        jnp.int32, (4, 128, 128), 1
    )
    gap = gap.reshape(512, 128)
    pre_lane = lax.broadcasted_iota(jnp.int32, (512, 128), 1)

    def attend_start(b):
        first = lax.dot_general(qs[b], pre_k[...], NT, preferred_element_type=F32) * scale
        first = jnp.where(pre_lane < 64, first, -1e30)
        pre_scores[b] = first
        top[b] = first

    def attend_scores(b, half):
        cols = slice(b * 128, (b + 1) * 128)

        def score(c, carry):
            block = lax.dot_general(
                qs[b],
                kv[0, pl.ds(2 * c, 2), :, cols].reshape(256, 128),
                NT,
                preferred_element_type=F32,
            )
            best = top[b]
            for r in range(2):
                source = ((x_lo + c // 4) % 2) * 8 + (z + 2 * c + r) % 8
                ahead = (x_lo * 8 + z - source) * 128
                part = jnp.where(gap <= ahead, block[:, r * 128 : (r + 1) * 128] * scale, -1e30)
                scores[b, c, :, r * 128 : (r + 1) * 128] = part
                best = jnp.maximum(best, part)
            top[b] = best
            return carry

        lax.fori_loop(half * 4, half * 4 + 4, score, 0)

    def attend_mix(b):
        cols = slice(b * 128, (b + 1) * 128)
        top[b] = jnp.broadcast_to(jnp.max(top[b], -1, keepdims=True), (512, 128))
        probs = jnp.exp(pre_scores[b] - top[b]).astype(BF)
        summed[...] = probs.astype(F32)
        weighted[...] = jnp.dot(probs, pre_v[...], preferred_element_type=F32)

        def mix(c, carry):
            peak = top[b]
            left = jnp.exp(scores[b, c, :, 0:128] - peak).astype(BF)
            right = jnp.exp(scores[b, c, :, 128:256] - peak).astype(BF)
            summed[...] += left.astype(F32) + right.astype(F32)
            weighted[...] += jnp.dot(
                jnp.concatenate([left, right], axis=1),
                kv[1, pl.ds(2 * c, 2), :, cols].reshape(256, 128),
                preferred_element_type=F32,
            )
            return carry

        lax.fori_loop(0, 8, mix, 0)
        result = weighted[...] / jnp.sum(summed[...], -1, keepdims=True)
        for h in range(4):
            for e in range(16):
                start = h * 128 + e * 8
                att[b, e % 2, (e // 2) % 4, e // 8, :, h * 128 : (h + 1) * 128] = result[
                    start : start + 8
                ]

        att_bf[0, b] = att[b].reshape(128, 512).astype(BF)
        return links.send(att_bf.at[0, b], att_bf.at[1, b], partner)

    attend_start(0)
    attend_start(1)
    shared[0].wait_recv()
    attend_scores(0, 0)
    hand_last(4)
    attend_scores(1, 0)
    w_step(0, 2)
    w_step(1, 2)
    shared[1].wait_recv()
    attend_scores(0, 1)
    attend_scores(1, 1)
    w_step(0, 3)
    swaps = [attend_mix(0)]
    w_step(1, 3)
    swaps.append(attend_mix(1))
    def half(p, c):
        rows = pl.ds(pl.multiple_of(c * 64, 64), 64)
        return att_bf[p, :, rows, :].reshape(128, 512)

    chunks = ((0, 7), (1, 6), (2, 5), (3, 4))
    core_moves, y_moves, x_moves = {}, {}, {}

    def project(j, p):
        for i, dz in enumerate(chunks[j]):
            cols = slice(i * 256, (i + 1) * 256)
            core_send[j, p, :, :, :, cols] = (
                jnp.dot(half(p, other), wts[dz], preferred_element_type=F32)
                .astype(BF)
                .reshape(2, 4, 16, 256)
            )
        core_moves[j, p] = links.send(core_send.at[j, p], core_recv.at[j, p], sibling)
        for i, dz in enumerate(chunks[j]):
            cols = slice(i * 256, (i + 1) * 256)
            own_term[j, p, :, :, :, cols] = jnp.dot(
                half(p, core), wts[dz], preferred_element_type=F32
            ).reshape(2, 4, 16, 256)

    def along_y(j, p):
        core_moves[j, p].wait_recv()
        both = own_term[j, p] + core_recv[j, p].astype(F32)
        own_term[j, p] = both
        y_send[j, p] = both.astype(BF)
        y_moves[j, p] = links.send_group(
            [
                (y_send.at[j, p, :, (y + d) % 4], y_recv.at[j, 4 - d, p], at(dy=d))
                for d in (2, 1, 3)
            ],
            y_recv.at[j, 1:4, p],
            y_recv.at[j, 1:4, p],
        )

    def along_x(j):
        own = own_term[j, :, :, y]
        y_moves[j, 0].wait_recv()
        y_moves[j, 1].wait_recv()
        for d in (1, 2, 3):
            own = own + y_recv[j, d].astype(F32)
        for p in range(2):
            for i in range(2):
                tile = jnp.concatenate(
                    [own[p, 0, i * 8 : i * 8 + 8], own[p, 1, i * 8 : i * 8 + 8]], axis=0
                )
                x_keep[j, p, i] = tile
                x_send[j, p, i] = tile.astype(BF)
        x_moves[j] = links.send_group(
            [
                (x_send.at[j, d % 2, ((x + d) % 4) // 2], x_recv.at[j, 4 - d], at(dx=d))
                for d in (2, 1, 3)
            ],
            x_recv.at[j, 1:4],
            x_recv.at[j, 1:4],
        )

    square = jnp.zeros((16, 128), F32)

    def join(j, square):
        x_moves[j].wait_recv()
        mine = x_keep[j, 0, x // 2] + x_recv[j, 2].astype(F32)
        theirs = x_recv[j, 1].astype(F32) + x_recv[j, 3].astype(F32)
        for i, dz in enumerate(chunks[j]):
            for side, part in ((x_lo, mine), (1 - x_lo, theirs)):
                where = pl.ds(pl.multiple_of((side * 8 + (z + dz) % 8) * 256, 256), 256)
                value = res[:, where] + part[:, i * 256 : (i + 1) * 256]
                hidden[:, where] = value
                value = value * value
                square = square + value[:, 0:128] + value[:, 128:256]
        return square

    project(0, 0)
    project(1, 0)
    along_y(0, 0)
    project(2, 0)
    along_y(1, 0)
    w_step(0, 4)
    w_step(1, 4)
    project(3, 0)
    along_y(2, 0)
    for copy in info_moves:
        copy.wait_recv()
    meta_a[...] = info_a[...]
    meta_b[0] = info_a[0]
    meta_b[1:4] = info_b[1:4]
    for swap in swaps:
        swap.wait_recv()

    project(0, 1)
    along_y(3, 0)
    project(1, 1)
    along_y(0, 1)
    project(2, 1)
    along_y(1, 1)
    project(3, 1)
    along_y(2, 1)
    along_x(0)
    along_y(3, 1)
    for j in (1, 2, 3):
        along_x(j)
    for j in range(4):
        square = join(j, square)
    mean = jnp.sum(square, -1, keepdims=True) * (1.0 / D)
    normed[...] = (hidden[...] * lax.rsqrt(mean + 1e-06) * gain_raw[...].reshape(1, D).astype(F32)).astype(BF)
    assert links.used <= ATT_SEMS
    links.finish()


def attention(*operands):
    vmem = pl.BlockSpec(memory_space=pltpu.VMEM)
    hbm = pl.BlockSpec(memory_space=pl.ANY)
    return pl.pallas_call(
        attn_kernel,
        out_shape=(
            jax.ShapeDtypeStruct((16, D), F32),
            jax.ShapeDtypeStruct((16, D), BF),
            jax.ShapeDtypeStruct((4, 256, 128), BF),
            jax.ShapeDtypeStruct((4, 256, 128), BF),
        ),
        in_specs=[hbm] * 10,
        out_specs=(vmem,) * 4,
        scratch_shapes=[
            pltpu.VMEM((128, 2, 512), BF),
            pltpu.VMEM((128, 2, 128), BF),
            pltpu.VMEM((128, 2, 128), BF),
            pltpu.VMEM((8, 2, D), BF),
            pltpu.VMEM((D,), BF),
            pltpu.VMEM((8, 2, TOPK), jnp.int32),
            pltpu.VMEM((8, 2, TOPK), F32),
            pltpu.VMEM((16, D), F32),
            pltpu.VMEM((2, 16, 128, 256), BF),
            pltpu.VMEM((8, 512, 256), BF),
            pltpu.VMEM((2, 512, 128), BF),
            pltpu.VMEM((128, 128), BF),
            pltpu.VMEM((128, 128), BF),
            pltpu.VMEM((2, 8, 512, 256), F32),
            pltpu.VMEM((2, 512, 128), F32),
            pltpu.VMEM((2, 512, 128), F32),
            pltpu.VMEM((512, 128), F32),
            pltpu.VMEM((512, 128), F32),
            pltpu.VMEM((2, 2, 4, 2, 8, 512), F32),
            pltpu.VMEM((2, 2, 128, 512), BF),
            pltpu.VMEM((4, 2, 2, 4, 16, 512), F32),
            pltpu.VMEM((4, 2, 2, 4, 16, 512), BF),
            pltpu.VMEM((4, 2, 2, 4, 16, 512), BF),
            pltpu.VMEM((4, 2, 2, 4, 16, 512), BF),
            pltpu.VMEM((4, 4, 2, 2, 16, 512), BF),
            pltpu.VMEM((4, 2, 2, 16, 512), F32),
            pltpu.VMEM((4, 2, 2, 16, 512), BF),
            pltpu.VMEM((4, 4, 16, 512), BF),
            pltpu.VMEM((4, 256, 128), BF),
            pltpu.VMEM((4, 256, 128), BF),
            pltpu.SemaphoreType.DMA((ATT_SEMS,)),
            pltpu.SemaphoreType.DMA((ATT_SEMS,)),
            pltpu.SemaphoreType.DMA((10,)),
        ],
        compiler_params=pltpu.CompilerParams(
            collective_id=2, has_side_effects=True, vmem_limit_bytes=60 * 2**20
        ),
        name="attention",
    )(*operands)


def shards(
    queries,
    keys,
    values,
    prefix_keys,
    prefix_values,
    out_weight,
    residual_in,
    norm_gain,
    expert_ids,
    route_weights,
    w_gate,
    w_up,
    w_down,
):
    hidden_state, normed, meta_a, meta_b = attention(
        queries,
        keys,
        values,
        prefix_keys,
        prefix_values,
        out_weight,
        residual_in,
        norm_gain,
        expert_ids,
        route_weights,
    )
    return moe(
        normed, meta_a, meta_b, hidden_state, w_gate[0, 0], w_up[0, 0], w_down[0, 0]
    )


def solution(mesh):
    in_specs = (
        P("seq", None, "expert"),
        P("seq", None, None),
        P("seq", None, None),
        P(),
        P(),
        P("expert", "seq"),
        P(("seq", "expert"), None, None),
        P(),
        P(("seq", "expert"), None, None),
        P(("seq", "expert"), None, None),
        P("seq", "expert", None, None),
        P("seq", "expert", None, None),
        P("seq", "expert", None, None),
    )
    out_specs = P(("seq", "expert"), None, None)
    return jax.shard_map(shards, mesh=mesh, in_specs=in_specs, out_specs=out_specs, check_vma=False)
```

```python
import math

import jax
import jax.numpy as jnp
from jax import lax
from jax.experimental import pallas as pl
from jax.experimental.pallas import tpu as pltpu
from jax.sharding import PartitionSpec as P

D = 4096
HD = 128
TOPK = 8

MESH = pl.DeviceIdType.MESH
BF = jnp.bfloat16
F32 = jnp.float32
NT = (((1,), (1,)), ((), ()))
ORDER = (0, 1, 3, 2)
SPOS = {0: 0, 1: 1, 3: 2, 2: 3}
MOE_SEMS = 91
FAR = (1, 2, 3)


def place():
    s = lax.axis_index("seq")
    e = lax.axis_index("expert")
    return (e // 8) * 2 + s // 8, (e // 2) % 4, s % 8, e % 2


def device(x, y, z, c):
    return ((x % 2) * 8 + z, ((x // 2) * 4 + y) * 2 + c)


class Links:
    def __init__(self, send_sems, recv_sems):
        self.send_sems = send_sems
        self.recv_sems = recv_sems
        self.used = 0
        self.open = []

    def copy(self, src, dst, peer, index):
        return pltpu.make_async_remote_copy(
            src_ref=src,
            dst_ref=dst,
            send_sem=self.send_sems.at[index],
            recv_sem=self.recv_sems.at[index],
            device_id=peer,
            device_id_type=MESH,
        )

    def send(self, src, dst, peer):
        copy = self.copy(src, dst, peer, self.used)
        self.used += 1
        copy.start()
        self.open.append(copy)
        return copy

    def send_group(self, copies, all_src, all_dst, peer=None):
        index = self.used
        self.used += 1
        for src, dst, to in copies:
            self.copy(src, dst, to, index).start()
        group = self.copy(all_src, all_dst, peer or copies[0][2], index)
        self.open.append(group)
        return group

    def more(self, index, src, dst, peer):
        self.copy(src, dst, peer, index).start()

    def finish(self):
        for copy in self.open:
            copy.wait_send()
        self.open = []


def greet(peers):
    barrier = pltpu.get_barrier_semaphore()
    for peer in peers:
        pl.semaphore_signal(barrier, inc=1, device_id=peer, device_id_type=MESH)
    return lambda: pl.semaphore_wait(barrier, len(peers))


def moe_kernel(
    normed,
    meta_a,
    meta_b,
    hidden,
    w_gate,
    w_up,
    w_down,
    out,
    mix,
    tok,
    stage,
    near,
    far,
    far_stage,
    slot,
    got,
    back,
    acc,
    hid,
    w_in,
    w_out,
    rank_mask,
    rank_mask_t,
    choose,
    scatter,
    part_send,
    part_recv,
    total,
    z_send,
    z_recv,
    far_total,
    far_send,
    far_plus,
    far_minus,
    line_send,
    line_recv,
    core_send,
    core_recv,
    send_sems,
    recv_sems,
    local_sems,
):
    x, y, z, core = place()
    other = 1 - core

    def at(dx=0, dy=0, dz=0, dc=0):
        return device((x + dx) % 4, (y + dy) % 4, (z + dz) % 8, (core + dc) % 2)

    def line(h, d):
        return at(dy=d) if h else at(dx=d)

    def toward(h, d, dc):
        return at(dx=d, dc=dc) if h else at(dy=d, dc=dc)

    sibling = at(dc=1)
    z_up, z_down = at(dz=1), at(dz=7)
    peers = [sibling] + [at(dz=d, dc=dc) for d in range(1, 8) for dc in (0, 1)]
    for d in (1, 2, 3):
        for dc in (0, 1):
            peers.append(at(dx=d, dc=dc))
            peers.append(at(dy=d, dc=dc))
    arrived = greet(peers)
    loads = [
        pltpu.make_async_copy(w_gate, w_in.at[:, 0:384], local_sems.at[0]),
        pltpu.make_async_copy(w_up, w_in.at[:, 384:768], local_sems.at[1]),
        pltpu.make_async_copy(w_down, w_out, local_sems.at[2]),
    ]
    for load in loads:
        load.start()

    def columns(k, h, c):
        return pl.ds(pl.multiple_of(k * 2048 + h * 1024 + c * 256, 256), 256)

    own_rows = pl.ds(pl.multiple_of(core * 16, 16), 16)
    for h in (0, 1):
        cols = slice(h * 256, (h + 1) * 256)
        stage[:, cols] = normed[:, columns(other, h, 0)]
        tok[own_rows, cols] = normed[:, columns(core, h, 0)]
        for c in FAR:
            far_stage[c - 1, h] = normed[:, columns(other, h, c)]
            far[c - 1, h, 0, 0, own_rows] = normed[:, columns(core, h, c)]

    links = Links(send_sems, recv_sems)
    arrived()
    def own_at(dz):
        return pl.ds(pl.multiple_of(dz * 32 + core * 16, 16), 16)

    swap = links.send(stage, tok.at[own_rows], sibling)
    ring = {}
    for d in (1, 7, 2, 6, 3, 5, 4):
        whole = tok.at[pl.ds((8 - d) * 32, 32)]
        ring[8 - d] = links.send_group(
            [
                (src, tok.at[own_at(8 - d)], at(dz=d, dc=dc))
                for dc, src in ((0, tok.at[own_rows]), (1, stage))
            ],
            whole,
            whole,
        )
    far_swap = links.send(far_stage, far.at[:, :, 0, 0, own_rows], sibling)
    swap.wait_recv()

    def rows(dz):
        return pl.ds(dz * 32, 32)

    dense = {}

    def spread(dz):
        r = rows(dz)
        dense[dz] = links.send_group(
            [
                (tok.at[r, h * 256 : (h + 1) * 256], near.at[h, 4 - d, r], line(h, d))
                for d in (2, 1, 3)
                for h in (0, 1)
            ],
            near.at[:, 1:4, r],
            near.at[:, 1:4, r],
        )

    spread(0)
    far_swap.wait_recv()
    far_line = links.send_group(
        [
            (far.at[:, h, 0, 0], far.at[:, h, 0, 4 - d], line(h, d))
            for d in (2, 1, 3)
            for h in (0, 1)
        ],
        far.at[:, :, 0, 1:4],
        far.at[:, :, 0, 1:4],
    )

    n = lax.broadcasted_iota(jnp.int32, (8, 48, 256), 1)
    t = lax.broadcasted_iota(jnp.int32, (8, 48, 256), 2)
    block = (n * 171) >> 9
    rank_mask[...] = (
        jnp.where(block == (t >> 4), n - 3 * block + 1, -1).astype(F32).reshape(384, 256)
    )
    r = lax.broadcasted_iota(jnp.int32, (256, 384), 1)
    t = lax.broadcasted_iota(jnp.int32, (256, 384), 0)
    n = r - 48 * ((r * 1366) >> 16)
    block = (n * 171) >> 9
    rank_mask_t[...] = jnp.where(block == (t >> 4), n - 3 * block + 1, -1).astype(F32)
    q = lax.broadcasted_iota(jnp.int32, (8, 48, 128), 0)
    lane = lax.broadcasted_iota(jnp.int32, (8, 48, 128), 2)
    step = q >> 1
    to_core = (core + (q & 1)) & 1
    to_y = (y + step) & 3
    to_x = (x + step) & 3
    half = z // 4
    expert_a = 4 * ((x // 2 * 4 + to_y) * 2 + to_core) + 2 * (x % 2) + half
    expert_b = 4 * (((to_x >> 1) * 4 + y) * 2 + to_core) + 2 * (to_x & 1) + half
    metas = (meta_a, meta_b)

    def one_hot(match):
        return jnp.where(match, 1.0, 0.0).astype(BF).reshape(384, 128)

    def masks(h, d):
        expert = expert_b if h else expert_a
        pick = one_hot(lane == expert)
        info = metas[h][d]
        found = lax.dot_general(pick, info, NT, preferred_element_type=F32)
        choose[h, d] = jnp.where(found == rank_mask[...], 1.0, 0.0).astype(BF)
        found = lax.dot_general(info, pick, NT, preferred_element_type=F32)
        scale = lax.dot_general(info, one_hot(lane == expert + 64), NT, preferred_element_type=F32)
        scatter[h, d] = jnp.where(found == rank_mask_t[...], scale, 0.0).astype(BF)

    far_up, far_down = {}, {}

    def far_start(c):
        piece = far.at[c - 1]
        far_up[c] = links.send(piece.at[:, 0], piece.at[:, 7], z_up)
        far_down[c] = links.send(piece.at[:, 0], piece.at[:, 1], z_down)

    def far_step(c, i):
        piece = far.at[c - 1]
        far_up[c].wait_recv()
        far_down[c].wait_recv()
        if i < 3:
            far_up[c] = links.send(piece.at[:, 8 - i], piece.at[:, 7 - i], z_up)
            far_down[c] = links.send(piece.at[:, i], piece.at[:, i + 1], z_down)
        elif i == 3:
            left, right = pl.ds(0, 2), pl.ds(2, 2)
            far_up[c] = links.send(piece.at[:, 5, left], piece.at[:, 4, left], z_up)
            far_down[c] = links.send(piece.at[:, 3, right], piece.at[:, 4, right], z_down)

    masks(0, 0)
    masks(1, 0)
    for dz in (7, 1):
        ring[dz].wait_recv()
        spread(dz)
    far_line.wait_recv()
    far_start(1)
    for dz in (6, 2, 5, 3, 4):
        ring[dz].wait_recv()
        spread(dz)
    far_start(2)
    masks(0, 1)
    masks(1, 1)
    masks(0, 3)
    far_step(1, 1)
    masks(1, 3)
    masks(0, 2)
    masks(1, 2)
    acc[...] = jnp.zeros_like(acc)

    def select(c, h, d):
        if c:
            tokens = far[c - 1, h, :, d].reshape(256, 256)
        elif d == 0:
            tokens = tok[:, h * 256 : (h + 1) * 256]
        else:
            tokens = near[h, d]
        picked = jnp.dot(choose[h, d], tokens, preferred_element_type=F32)
        slot[c, h, SPOS[d]] = picked.astype(BF).reshape(8, 48, 256)

    moved, kept = {}, {}

    def dispatch(c, h):
        for d in (0, 1, 3, 2):
            select(c, h, d)
        copies = []
        for d in (2, 1, 3, 0):
            for dc in (0, 1):
                src = slot.at[c, h, :, d * 2 + dc]
                dst = got.at[c, h, ((4 - d) % 4) * 2 + dc]
                if d == 0 and dc == 0:
                    kept[c, h] = pltpu.make_async_copy(src, dst, local_sems.at[3 + c * 2 + h])
                    kept[c, h].start()
                else:
                    copies.append((src, dst, toward(h, d, dc)))
        moved[c, h] = links.send_group(copies, slot.at[c, h, :, 1:8], got.at[c, h, 1:8])

    def expert_in(c, h):
        kept[c, h].wait()
        moved[c, h].wait_recv()
        for d in (0, 1, 3, 2):
            term = 0
            for dc in (0, 1):
                k = (core + dc) % 2
                term = term + jnp.dot(
                    got[c, h, d * 2 + dc].reshape(192, 256),
                    w_in[columns(k, h, c), :],
                    preferred_element_type=F32,
                )
            if h == 0:
                acc[:, SPOS[d]] += term.reshape(4, 48, 768)
            else:
                acc[SPOS[d]] += term.reshape(4, 48, 768)

    for dz in range(8):
        dense[dz].wait_recv()
    dispatch(0, 0)
    far_step(1, 2)
    dispatch(0, 1)
    far_step(2, 1)
    far_step(1, 3)
    far_start(3)
    for load in loads:
        load.wait()
    far_step(2, 2)
    far_step(1, 4)
    dispatch(1, 0)
    far_step(2, 3)
    far_step(3, 1)
    dispatch(1, 1)
    expert_in(0, 0)
    far_step(2, 4)
    far_step(3, 2)
    dispatch(2, 0)
    dispatch(2, 1)
    far_step(3, 3)
    expert_in(0, 1)
    far_step(3, 4)
    dispatch(3, 0)
    dispatch(3, 1)
    for c in FAR:
        for h in (0, 1):
            expert_in(c, h)
    for i in range(4):
        gate = acc[i, :, :, 0:384]
        hid[i] = (gate / (1.0 + jnp.exp(-gate)) * acc[i, :, :, 384:768]).astype(BF)

    returned = {}

    def expert_out(c, h):
        index = links.used
        returned[c, h] = links.send_group(
            [], got.at[c, h, 1:8], back.at[c, h, :, 1:8], sibling
        )
        for d in (2, 1, 3, 0):
            rows_in = hid[:, SPOS[d]] if h == 0 else hid[SPOS[d]]
            for dc in (0, 1):
                k = (core + dc) % 2
                block_out = (
                    jnp.dot(
                        rows_in.reshape(192, 384),
                        w_out[:, columns(k, h, c)],
                        preferred_element_type=F32,
                    )
                    .astype(BF)
                    .reshape(4, 48, 256)
                )
                if d == 0 and dc == 0:
                    back[c, h, :, 0] = block_out
                    continue
                target = ((4 - d) % 4) * 2 + dc
                got[c, h, d * 2 + dc] = block_out
                links.more(
                    index, got.at[c, h, d * 2 + dc], back.at[c, h, :, target], toward(h, d, dc)
                )

    def combine(c, h, d):
        return jnp.dot(
            scatter[h, d], back[c, h, SPOS[d]].reshape(384, 256), preferred_element_type=F32
        )

    def all_back(c, h):
        returned[c, h].wait_recv()

    def far_open(c):
        for h in (0, 1):
            all_back(c, h)
            for d in range(4):
                far_total[c - 1, h, d] = combine(c, h, d)
        send, left, right = far_send.at[c - 1], pl.ds(0, 2), pl.ds(2, 2)
        send[:, 4] = far_total[c - 1, :, :, 128:160].astype(BF)
        far_up[c] = links.send(send.at[:, 4, left], far_plus.at[c - 1, 3, :, left], z_up)
        far_down[c] = links.send(send.at[:, 4, right], far_minus.at[c - 1, 3, :, right], z_down)

    def far_return(c, i):
        rest = 8 - i
        left, right = slice(0, 2), slice(2, 4)
        send, plus, minus = far_send.at[c - 1], far_plus.at[c - 1], far_minus.at[c - 1]

        def mine(dz, span=slice(0, 4)):
            return far_total[c - 1, :, span, dz * 32 : dz * 32 + 32]

        far_up[c].wait_recv()
        if i == 3:
            send[:, i, left] = (mine(i, left) + plus[i, :, left].astype(F32)).astype(BF)
            send[:, i, right] = mine(i, right).astype(BF)
        else:
            send[:, i] = (mine(i) + plus[i].astype(F32)).astype(BF)
        far_up[c] = links.send(send.at[:, i], plus.at[i - 1], z_up)
        far_down[c].wait_recv()
        if i == 3:
            send[:, rest, left] = mine(rest, left).astype(BF)
            send[:, rest, right] = (mine(rest, right) + minus[i, :, right].astype(F32)).astype(BF)
        else:
            send[:, rest] = (mine(rest) + minus[i].astype(F32)).astype(BF)
        far_down[c] = links.send(send.at[:, rest], minus.at[i - 1], z_down)

    line_moves = {}

    def far_finish(c):
        far_up[c].wait_recv()
        far_down[c].wait_recv()
        ends = (
            far_total[c - 1, :, :, 0:32]
            + far_plus[c - 1, 0].astype(F32)
            + far_minus[c - 1, 0].astype(F32)
        )
        line_send[c - 1] = ends.astype(BF)
        line_moves[c] = links.send_group(
            [
                (line_send.at[c - 1, h, d], line_recv.at[c - 1, h, (4 - d) % 4], line(h, d))
                for d in (2, 1, 3)
                for h in (0, 1)
            ],
            line_send.at[c - 1, :, 1:4],
            line_recv.at[c - 1, :, 1:4],
        )
        far_total[c - 1, :, 0, 0:32] = ends[:, 0]

    def far_join(c):
        line_moves[c].wait_recv()
        for d in (1, 2, 3):
            far_total[c - 1, :, 0, 0:32] += line_recv[c - 1, :, d].astype(F32)

    parts = {}

    def near_part(h):
        all_back(0, h)
        index = links.used
        parts[h] = links.send_group([], part_send.at[h, 1:4], part_recv.at[h, 1:4], line(h, 1))
        for d in (2, 1, 3):
            part_send[h, d] = combine(0, h, d).astype(BF)
            links.more(index, part_send.at[h, d], part_recv.at[h, 4 - d], line(h, d))
        total[:, h * 256 : (h + 1) * 256] = combine(0, h, 0)

    def near_join(h):
        parts[h].wait_recv()
        rest = part_recv[h, 1].astype(F32) + part_recv[h, 2].astype(F32)
        total[:, h * 256 : (h + 1) * 256] += rest + part_recv[h, 3].astype(F32)

    def z_return():
        z_send[...] = total[...].reshape(8, 2, 16, 512).astype(BF)
        far_side = links.send_group(
            [
                (z_send.at[d, (core + dc) % 2], z_recv.at[8 - d, dc], at(dz=d, dc=dc))
                for d in (4, 3, 5, 2, 6, 1, 7)
                for dc in (0, 1)
            ],
            z_send.at[1:8],
            z_recv.at[1:8],
        )
        return far_side, links.send(z_send.at[0, other], z_recv.at[0, 1], sibling)

    for c in (1, 2):
        for h in (0, 1):
            expert_out(c, h)
    far_open(1)
    expert_out(3, 0)
    far_return(1, 3)
    expert_out(3, 1)
    far_return(1, 2)
    far_open(2)
    far_return(1, 1)
    expert_out(0, 0)
    far_return(2, 3)
    expert_out(0, 1)
    far_finish(1)
    far_return(2, 2)
    far_open(3)
    far_return(2, 1)
    far_return(3, 3)
    near_part(0)
    near_part(1)
    far_return(3, 2)
    far_finish(2)
    far_return(3, 1)
    near_join(0)
    near_join(1)
    ending = z_return()
    far_join(1)
    far_join(2)
    far_finish(3)
    far_join(3)
    other_rows = pl.ds(pl.multiple_of(other * 16, 16), 16)
    for h in (0, 1):
        for c in FAR:
            core_send[h * 3 + c - 1] = far_total[c - 1, h, 0, other_rows].astype(BF)
    swap = links.send(core_send, core_recv, sibling)
    for h in (0, 1):
        for c in FAR:
            mix[:, columns(core, h, c)] = far_total[c - 1, h, 0, own_rows]
    swap.wait_recv()
    for h in (0, 1):
        for c in FAR:
            mix[:, columns(other, h, c)] = core_recv[h * 3 + c - 1].astype(F32)
    for copy in ending:
        copy.wait_recv()
    ends = total[own_rows]
    beside = z_recv[0, 1].astype(F32)
    for d in range(1, 8):
        ends = ends + z_recv[d, 0].astype(F32)
        beside = beside + z_recv[d, 1].astype(F32)
    for h in (0, 1):
        mix[:, columns(core, h, 0)] = ends[:, h * 256 : (h + 1) * 256]
        mix[:, columns(other, h, 0)] = beside[:, h * 256 : (h + 1) * 256]
    result = hidden[...] + mix[...]
    out[...] = jnp.stack([result[0:8], result[8:16]], axis=1).astype(BF)
    assert links.used <= MOE_SEMS
    links.finish()


def moe(*operands):
    vmem = pl.BlockSpec(memory_space=pltpu.VMEM)
    hbm = pl.BlockSpec(memory_space=pl.ANY)
    return pl.pallas_call(
        moe_kernel,
        out_shape=jax.ShapeDtypeStruct((8, 2, D), BF),
        in_specs=[vmem, vmem, vmem, vmem, hbm, hbm, hbm],
        out_specs=vmem,
        scratch_shapes=[
            pltpu.VMEM((16, D), F32),
            pltpu.VMEM((256, 512), BF),
            pltpu.VMEM((16, 512), BF),
            pltpu.VMEM((2, 4, 256, 256), BF),
            pltpu.VMEM((3, 2, 8, 4, 32, 256), BF),
            pltpu.VMEM((3, 2, 16, 256), BF),
            pltpu.VMEM((4, 2, 4, 8, 48, 256), BF),
            pltpu.VMEM((4, 2, 8, 4, 48, 256), BF),
            pltpu.VMEM((4, 2, 4, 8, 48, 256), BF),
            pltpu.VMEM((4, 4, 48, 768), F32),
            pltpu.VMEM((4, 4, 48, 384), BF),
            pltpu.VMEM((4096, 768), BF),
            pltpu.VMEM((384, 4096), BF),
            pltpu.VMEM((384, 256), F32),
            pltpu.VMEM((256, 384), F32),
            pltpu.VMEM((2, 4, 384, 256), BF),
            pltpu.VMEM((2, 4, 256, 384), BF),
            pltpu.VMEM((2, 4, 256, 256), BF),
            pltpu.VMEM((2, 4, 256, 256), BF),
            pltpu.VMEM((256, 512), F32),
            pltpu.VMEM((8, 2, 16, 512), BF),
            pltpu.VMEM((8, 2, 16, 512), BF),
            pltpu.VMEM((3, 2, 4, 256, 256), F32),
            pltpu.VMEM((3, 2, 8, 4, 32, 256), BF),
            pltpu.VMEM((3, 4, 2, 4, 32, 256), BF),
            pltpu.VMEM((3, 4, 2, 4, 32, 256), BF),
            pltpu.VMEM((3, 2, 4, 32, 256), BF),
            pltpu.VMEM((3, 2, 4, 32, 256), BF),
            pltpu.VMEM((6, 16, 256), BF),
            pltpu.VMEM((6, 16, 256), BF),
            pltpu.SemaphoreType.DMA((MOE_SEMS,)),
            pltpu.SemaphoreType.DMA((MOE_SEMS,)),
            pltpu.SemaphoreType.DMA((16,)),
        ],
        compiler_params=pltpu.CompilerParams(
            collective_id=1, has_side_effects=True, vmem_limit_bytes=60 * 2**20
        ),
        name="moe",
    )(*operands)


ATT_SEMS = 75


def attn_kernel(
    queries,
    keys,
    values,
    prefix_keys,
    prefix_values,
    out_weight,
    residual,
    gain,
    ids_in,
    gates_in,
    hidden,
    normed,
    meta_a,
    meta_b,
    q_raw,
    k_raw,
    v_raw,
    res_raw,
    gain_raw,
    ids,
    gates,
    res,
    kv,
    wts,
    qs,
    pre_k,
    pre_v,
    scores,
    pre_scores,
    top,
    summed,
    weighted,
    att,
    att_bf,
    own_term,
    core_send,
    core_recv,
    y_send,
    y_recv,
    x_keep,
    x_send,
    x_recv,
    info_a,
    info_b,
    send_sems,
    recv_sems,
    local_sems,
):
    x, y, z, core = place()
    other = 1 - core
    x_lo = x % 2
    kv_head = (lax.axis_index("expert")) // 4

    def at(dx=0, dy=0, dz=0, dc=0):
        return device((x + dx) % 4, (y + dy) % 4, (z + dz) % 8, (core + dc) % 2)

    sibling = at(dc=1)
    partner = device(x + 1 - 2 * x_lo, y, z, core)
    y_partner = device(x, y + 1 - 2 * (y % 2), z, core)
    mine = pl.ds(pl.multiple_of((y % 2) * 64, 64), 64)
    theirs = pl.ds(pl.multiple_of((1 - y % 2) * 64, 64), 64)
    z_up, z_down = at(dz=1), at(dz=7)
    peers = [sibling, z_up, z_down, at(dz=2), at(dz=6)]
    for d in (1, 2, 3):
        peers.append(at(dx=d))
        peers.append(at(dy=d))
    arrived = greet(peers)
    head_cols = pl.ds(pl.multiple_of(kv_head * 128, 128), 128)
    loads = [
        pltpu.make_async_copy(src, dst, local_sems.at[i])
        for i, (src, dst) in enumerate(
            (
                (keys.at[:, :, head_cols], k_raw),
                (values.at[:, :, head_cols], v_raw),
                (ids_in, ids),
                (gates_in, gates),
                (out_weight, wts.at[0]),
                (queries, q_raw),
                (prefix_keys.at[:, head_cols], pre_k.at[0:64]),
                (prefix_values.at[:, head_cols], pre_v.at[0:64]),
                (residual, res_raw),
                (gain, gain_raw),
            )
        )
    ]
    for load in loads:
        load.start()
    for load in loads[:4]:
        load.wait()
    for b in range(2):
        kv[core, 0, :, b * 128 : (b + 1) * 128] = jnp.where(
            core == 0, k_raw[:, b, :].astype(F32), v_raw[:, b, :].astype(F32)
        ).astype(BF)
    token_ids = jnp.concatenate([ids[:, 0, :], ids[:, 1, :]], axis=0)
    token_gates = jnp.concatenate([gates[:, 0, :], gates[:, 1, :]], axis=0)
    lane = lax.broadcasted_iota(jnp.int32, (16, 128), 1)
    chosen = jnp.zeros((16, 128), F32)
    weight = jnp.zeros((16, 128), F32)
    for j in range(TOPK):
        column = token_ids[:, j : j + 1]
        chosen = chosen + jnp.where(lane == column, 1.0, 0.0)
        weight = weight + jnp.where(lane == column + 64, token_gates[:, j : j + 1], 0.0)
    row_i = lax.broadcasted_iota(jnp.int32, (16, 16), 0)
    col_i = lax.broadcasted_iota(jnp.int32, (16, 16), 1)
    lower = jnp.where(col_i <= row_i, 1.0, 0.0).astype(BF)
    rank = jnp.dot(lower, chosen.astype(BF), preferred_element_type=F32)
    own_rows = pl.ds(pl.multiple_of(core * 16, 16), 16)
    info_a[0, own_rows] = (rank * chosen + weight).astype(BF)

    links = Links(send_sems, recv_sems)
    arrived()

    def lines(dz):
        return pl.ds(dz * 32, 32)

    info = links.send(info_a.at[0, own_rows], info_a.at[0, own_rows], sibling)
    info_up, info_down = {}, {}

    def info_step(i):
        if i:
            info_up[i].wait_recv()
            info_down[i].wait_recv()
        else:
            info.wait_recv()
        if i < 3:
            src = info_a.at[0, lines((8 - i) % 8)]
            info_up[i + 1] = links.send(src, info_a.at[0, lines(7 - i)], z_up)
            info_down[i + 1] = links.send(
                info_a.at[0, lines(i)], info_a.at[0, lines(i + 1)], z_down
            )
        elif i == 3:
            low, high = pl.ds(4 * 32, 16), pl.ds(4 * 32 + 16, 16)
            info_up[4] = links.send(info_a.at[0, pl.ds(5 * 32, 16)], info_a.at[0, low], z_up)
            info_down[4] = links.send(info_a.at[0, pl.ds(3 * 32 + 16, 16)], info_a.at[0, high], z_down)


    across, beside = {}, {}
    sharing = links.used
    shared = [
        links.send_group([], kv.at[core, pl.ds(i * 8, 8)], kv.at[core, pl.ds(i * 8, 8)], sibling)
        for i in (0, 1)
    ]

    def share(block, rows=pl.ds(0, 128)):
        piece = kv.at[core, block, rows]
        links.more(sharing + block // 8, piece, piece, sibling)

    def hand_on(dz):
        share(dz)
        across[dz] = links.send(kv.at[core, dz, mine], kv.at[core, 8 + dz, mine], partner)

    def hand_over(dz):
        across[dz].wait_recv()
        piece = kv.at[core, 8 + dz, mine]
        beside[dz] = links.send(piece, piece, y_partner)
        share(8 + dz, mine)

    def hand_last(dz):
        beside[dz].wait_recv()
        share(8 + dz, theirs)

    w_up, w_down = {}, {}

    def w_start(s):
        r = pl.ds(s * 256, 256)
        w_up[s] = links.send(wts.at[0, r], wts.at[7, r], z_up)
        w_down[s] = links.send(wts.at[0, r], wts.at[1, r], z_down)

    def w_step(s, i):
        r = pl.ds(s * 256, 256)
        w_up[s].wait_recv()
        w_down[s].wait_recv()
        if i < 3:
            w_up[s] = links.send(wts.at[8 - i, r], wts.at[7 - i, r], z_up)
            w_down[s] = links.send(wts.at[i, r], wts.at[i + 1, r], z_down)
        elif i == 3:
            first, second = pl.ds(s * 256, 128), pl.ds(s * 256 + 128, 128)
            w_up[s] = links.send(wts.at[5, first], wts.at[4, first], z_up)
            w_down[s] = links.send(wts.at[3, second], wts.at[4, second], z_down)

    low, high = pl.ds(0, 64), pl.ds(64, 64)
    ring = {}
    for d in (1, 7, 2, 6):
        ring[8 - d] = links.send(kv.at[core, 0], kv.at[core, 8 - d], at(dz=d))
    hand_on(0)
    info_step(0)

    for load in loads[4:]:
        load.wait()
    for b in range(2):
        for h in range(4):
            qs[b, h * 128 : (h + 1) * 128, :] = q_raw[:, b, h * 128 : (h + 1) * 128]
    pre_k[64:128] = jnp.zeros((64, 128), BF)
    pre_v[64:128] = jnp.zeros((64, 128), BF)

    for dz in (7, 1):
        ring[dz].wait_recv()
        hand_on(dz)
    w_start(0)
    w_start(1)
    for dz, part, peer, far in ((6, low, z_up, at(dz=2)), (2, high, z_down, at(dz=6))):
        ring[dz].wait_recv()
        ring[5 if dz == 6 else 3] = links.send(
            kv.at[core, dz], kv.at[core, 5 if dz == 6 else 3], peer
        )
        ring[4, dz] = links.send(kv.at[core, dz, part], kv.at[core, 4, part], far)
        hand_on(dz)
    hand_over(0)
    info_step(1)
    hand_over(7)
    hand_over(1)
    hand_last(0)
    info_step(2)
    for dz in (5, 3):
        ring[dz].wait_recv()
        hand_on(dz)
    ring[4, 6].wait_recv()
    ring[4, 2].wait_recv()
    hand_on(4)
    hand_over(6)
    hand_over(2)
    hand_last(7)
    hand_last(1)
    w_step(0, 1)
    info_step(3)
    hand_over(5)
    hand_over(3)
    hand_last(6)
    hand_last(2)
    w_step(1, 1)
    hand_over(4)
    info_step(4)
    hand_last(5)
    hand_last(3)
    info_moves = [
        links.send_group(
            [(info_a.at[0], dst.at[4 - d], at(**{axis: d})) for d in (1, 2, 3)],
            dst.at[1:4],
            dst.at[1:4],
        )
        for dst, axis in ((info_a, "dx"), (info_b, "dy"))
    ]
    for b in range(2):
        res[b * 8 : (b + 1) * 8] = res_raw[:, b, :].astype(F32)

    scale = 1.0 / math.sqrt(HD)
    gap = lax.broadcasted_iota(jnp.int32, (4, 128, 128), 2) - lax.broadcasted_iota(
        jnp.int32, (4, 128, 128), 1
    )
    gap = gap.reshape(512, 128)
    pre_lane = lax.broadcasted_iota(jnp.int32, (512, 128), 1)

    def attend_start(b):
        first = lax.dot_general(qs[b], pre_k[...], NT, preferred_element_type=F32) * scale
        first = jnp.where(pre_lane < 64, first, -1e30)
        pre_scores[b] = first
        top[b] = first

    def attend_scores(b, half):
        cols = slice(b * 128, (b + 1) * 128)

        def score(c, carry):
            block = lax.dot_general(
                qs[b],
                kv[0, pl.ds(2 * c, 2), :, cols].reshape(256, 128),
                NT,
                preferred_element_type=F32,
            )
            best = top[b]
            for r in range(2):
                source = ((x_lo + c // 4) % 2) * 8 + (z + 2 * c + r) % 8
                ahead = (x_lo * 8 + z - source) * 128
                part = jnp.where(gap <= ahead, block[:, r * 128 : (r + 1) * 128] * scale, -1e30)
                scores[b, c, :, r * 128 : (r + 1) * 128] = part
                best = jnp.maximum(best, part)
            top[b] = best
            return carry

        lax.fori_loop(half * 4, half * 4 + 4, score, 0)

    def attend_mix(b):
        cols = slice(b * 128, (b + 1) * 128)
        top[b] = jnp.broadcast_to(jnp.max(top[b], -1, keepdims=True), (512, 128))
        probs = jnp.exp(pre_scores[b] - top[b]).astype(BF)
        summed[...] = probs.astype(F32)
        weighted[...] = jnp.dot(probs, pre_v[...], preferred_element_type=F32)

        def mix(c, carry):
            peak = top[b]
            left = jnp.exp(scores[b, c, :, 0:128] - peak).astype(BF)
            right = jnp.exp(scores[b, c, :, 128:256] - peak).astype(BF)
            summed[...] += left.astype(F32) + right.astype(F32)
            weighted[...] += jnp.dot(
                jnp.concatenate([left, right], axis=1),
                kv[1, pl.ds(2 * c, 2), :, cols].reshape(256, 128),
                preferred_element_type=F32,
            )
            return carry

        lax.fori_loop(0, 8, mix, 0)
        result = weighted[...] / jnp.sum(summed[...], -1, keepdims=True)
        for h in range(4):
            for e in range(16):
                start = h * 128 + e * 8
                att[b, e % 2, (e // 2) % 4, e // 8, :, h * 128 : (h + 1) * 128] = result[
                    start : start + 8
                ]

        att_bf[0, b] = att[b].reshape(128, 512).astype(BF)
        return links.send(att_bf.at[0, b], att_bf.at[1, b], partner)

    attend_start(0)
    attend_start(1)
    shared[0].wait_recv()
    attend_scores(0, 0)
    hand_last(4)
    attend_scores(1, 0)
    w_step(0, 2)
    w_step(1, 2)
    shared[1].wait_recv()
    attend_scores(0, 1)
    attend_scores(1, 1)
    w_step(0, 3)
    swaps = [attend_mix(0)]
    w_step(1, 3)
    swaps.append(attend_mix(1))
    def half(p, c):
        rows = pl.ds(pl.multiple_of(c * 64, 64), 64)
        return att_bf[p, :, rows, :].reshape(128, 512)

    chunks = ((0, 7), (1, 6), (2, 5), (3, 4))
    core_moves, y_moves, x_moves = {}, {}, {}

    def project(j, p):
        for i, dz in enumerate(chunks[j]):
            cols = slice(i * 256, (i + 1) * 256)
            core_send[j, p, :, :, :, cols] = (
                jnp.dot(half(p, other), wts[dz], preferred_element_type=F32)
                .astype(BF)
                .reshape(2, 4, 16, 256)
            )
        core_moves[j, p] = links.send(core_send.at[j, p], core_recv.at[j, p], sibling)
        for i, dz in enumerate(chunks[j]):
            cols = slice(i * 256, (i + 1) * 256)
            own_term[j, p, :, :, :, cols] = jnp.dot(
                half(p, core), wts[dz], preferred_element_type=F32
            ).reshape(2, 4, 16, 256)

    def along_y(j, p):
        core_moves[j, p].wait_recv()
        both = own_term[j, p] + core_recv[j, p].astype(F32)
        own_term[j, p] = both
        y_send[j, p] = both.astype(BF)
        y_moves[j, p] = links.send_group(
            [
                (y_send.at[j, p, :, (y + d) % 4], y_recv.at[j, 4 - d, p], at(dy=d))
                for d in (2, 1, 3)
            ],
            y_recv.at[j, 1:4, p],
            y_recv.at[j, 1:4, p],
        )

    def along_x(j):
        own = own_term[j, :, :, y]
        y_moves[j, 0].wait_recv()
        y_moves[j, 1].wait_recv()
        for d in (1, 2, 3):
            own = own + y_recv[j, d].astype(F32)
        for p in range(2):
            for i in range(2):
                tile = jnp.concatenate(
                    [own[p, 0, i * 8 : i * 8 + 8], own[p, 1, i * 8 : i * 8 + 8]], axis=0
                )
                x_keep[j, p, i] = tile
                x_send[j, p, i] = tile.astype(BF)
        x_moves[j] = links.send_group(
            [
                (x_send.at[j, d % 2, ((x + d) % 4) // 2], x_recv.at[j, 4 - d], at(dx=d))
                for d in (2, 1, 3)
            ],
            x_recv.at[j, 1:4],
            x_recv.at[j, 1:4],
        )

    square = jnp.zeros((16, 128), F32)

    def join(j, square):
        x_moves[j].wait_recv()
        mine = x_keep[j, 0, x // 2] + x_recv[j, 2].astype(F32)
        theirs = x_recv[j, 1].astype(F32) + x_recv[j, 3].astype(F32)
        for i, dz in enumerate(chunks[j]):
            for side, part in ((x_lo, mine), (1 - x_lo, theirs)):
                where = pl.ds(pl.multiple_of((side * 8 + (z + dz) % 8) * 256, 256), 256)
                value = res[:, where] + part[:, i * 256 : (i + 1) * 256]
                hidden[:, where] = value
                value = value * value
                square = square + value[:, 0:128] + value[:, 128:256]
        return square

    project(0, 0)
    project(1, 0)
    along_y(0, 0)
    project(2, 0)
    along_y(1, 0)
    w_step(0, 4)
    w_step(1, 4)
    project(3, 0)
    along_y(2, 0)
    for copy in info_moves:
        copy.wait_recv()
    meta_a[...] = info_a[...]
    meta_b[0] = info_a[0]
    meta_b[1:4] = info_b[1:4]
    for swap in swaps:
        swap.wait_recv()

    project(0, 1)
    along_y(3, 0)
    project(1, 1)
    along_y(0, 1)
    project(2, 1)
    along_y(1, 1)
    project(3, 1)
    along_y(2, 1)
    along_x(0)
    along_y(3, 1)
    for j in (1, 2, 3):
        along_x(j)
        square = join(j - 1, square)
    square = join(3, square)
    mean = jnp.sum(square, -1, keepdims=True) * (1.0 / D)
    normed[...] = (hidden[...] * lax.rsqrt(mean + 1e-06) * gain_raw[...].reshape(1, D).astype(F32)).astype(BF)
    assert links.used <= ATT_SEMS
    links.finish()


def attention(*operands):
    vmem = pl.BlockSpec(memory_space=pltpu.VMEM)
    hbm = pl.BlockSpec(memory_space=pl.ANY)
    return pl.pallas_call(
        attn_kernel,
        out_shape=(
            jax.ShapeDtypeStruct((16, D), F32),
            jax.ShapeDtypeStruct((16, D), BF),
            jax.ShapeDtypeStruct((4, 256, 128), BF),
            jax.ShapeDtypeStruct((4, 256, 128), BF),
        ),
        in_specs=[hbm] * 10,
        out_specs=(vmem,) * 4,
        scratch_shapes=[
            pltpu.VMEM((128, 2, 512), BF),
            pltpu.VMEM((128, 2, 128), BF),
            pltpu.VMEM((128, 2, 128), BF),
            pltpu.VMEM((8, 2, D), BF),
            pltpu.VMEM((D,), BF),
            pltpu.VMEM((8, 2, TOPK), jnp.int32),
            pltpu.VMEM((8, 2, TOPK), F32),
            pltpu.VMEM((16, D), F32),
            pltpu.VMEM((2, 16, 128, 256), BF),
            pltpu.VMEM((8, 512, 256), BF),
            pltpu.VMEM((2, 512, 128), BF),
            pltpu.VMEM((128, 128), BF),
            pltpu.VMEM((128, 128), BF),
            pltpu.VMEM((2, 8, 512, 256), F32),
            pltpu.VMEM((2, 512, 128), F32),
            pltpu.VMEM((2, 512, 128), F32),
            pltpu.VMEM((512, 128), F32),
            pltpu.VMEM((512, 128), F32),
            pltpu.VMEM((2, 2, 4, 2, 8, 512), F32),
            pltpu.VMEM((2, 2, 128, 512), BF),
            pltpu.VMEM((4, 2, 2, 4, 16, 512), F32),
            pltpu.VMEM((4, 2, 2, 4, 16, 512), BF),
            pltpu.VMEM((4, 2, 2, 4, 16, 512), BF),
            pltpu.VMEM((4, 2, 2, 4, 16, 512), BF),
            pltpu.VMEM((4, 4, 2, 2, 16, 512), BF),
            pltpu.VMEM((4, 2, 2, 16, 512), F32),
            pltpu.VMEM((4, 2, 2, 16, 512), BF),
            pltpu.VMEM((4, 4, 16, 512), BF),
            pltpu.VMEM((4, 256, 128), BF),
            pltpu.VMEM((4, 256, 128), BF),
            pltpu.SemaphoreType.DMA((ATT_SEMS,)),
            pltpu.SemaphoreType.DMA((ATT_SEMS,)),
            pltpu.SemaphoreType.DMA((10,)),
        ],
        compiler_params=pltpu.CompilerParams(
            collective_id=2, has_side_effects=True, vmem_limit_bytes=60 * 2**20
        ),
        name="attention",
    )(*operands)


def shards(
    queries,
    keys,
    values,
    prefix_keys,
    prefix_values,
    out_weight,
    residual_in,
    norm_gain,
    expert_ids,
    route_weights,
    w_gate,
    w_up,
    w_down,
):
    hidden_state, normed, meta_a, meta_b = attention(
        queries,
        keys,
        values,
        prefix_keys,
        prefix_values,
        out_weight,
        residual_in,
        norm_gain,
        expert_ids,
        route_weights,
    )
    return moe(
        normed, meta_a, meta_b, hidden_state, w_gate[0, 0], w_up[0, 0], w_down[0, 0]
    )


def solution(mesh):
    in_specs = (
        P("seq", None, "expert"),
        P("seq", None, None),
        P("seq", None, None),
        P(),
        P(),
        P("expert", "seq"),
        P(("seq", "expert"), None, None),
        P(),
        P(("seq", "expert"), None, None),
        P(("seq", "expert"), None, None),
        P("seq", "expert", None, None),
        P("seq", "expert", None, None),
        P("seq", "expert", None, None),
    )
    out_specs = P(("seq", "expert"), None, None)
    return jax.shard_map(shards, mesh=mesh, in_specs=in_specs, out_specs=out_specs, check_vma=False)
```
